256 devices in a mesh: dp: 2 (over y_lo), space: 16 (over z, y_hi), chan: 8 (over x, core).
Axes of the slice: x: 4, y: 4 (y_hi: 2, y_lo: 2; y = y_hi * 2 + y_lo), z: 8, core: 2. Of those that a mesh axis runs over, the one named last changes fastest.
Arguments:
- volumes: bfloat16 [2, 32, 512, 1024], P('dp', 'space', 'chan'), may hold values from -6 to 6
- kernel: bfloat16 [512, 13824], P('chan'), may hold values from -0.15625 to 0.15625
- bias: float32 [512], P('chan'), may hold values from -3 to 3
- act_grad: bfloat16 [2, 16, 512, 256], P('dp', 'space', 'chan'), may hold values from -6 to 6
Outputs:
- activation: bfloat16 [2, 16, 512, 256], P('dp', 'space', 'chan')
- grad_x: bfloat16 [2, 32, 512, 1024], P('dp', 'space', 'chan')
- grad_w: float32 [512, 13824], P('chan')
- grad_b: float32 [512], P('chan')
The draws below stay inside these ranges and needn't reach their ends.
All inputs are finite; a program needn't handle non-finite values.
Results may differ from the reference program's by a relative error of at most 0.005.
Values may be sent and summed in bfloat16 or wider, within the bound.
No kernel may reach another device: no remote copies, remote signals or barrier semaphores. Data moves between devices by JAX's collectives and lax.ppermute only.
A program may use at most 64 MiB of HBM per device.

```python
import jax
import jax.numpy as jnp
from jax import lax

CIN = 512
COUT = 512
GRID = 32
VOLUMES = 2
GX = 32
OX = 16
OG = 16
N_CHAN = 8


def shard_levels(key, shape, split, low, top_value):
    factor_of = 1.0
    for position, blocks in split:
        draws = jax.random.uniform(jax.random.fold_in(jax.random.fold_in(key, 6), position), (blocks,), jnp.float32, low / len(split), top_value / len(split))
        factor_of = factor_of * jnp.repeat(jnp.exp(draws), shape[position] // blocks).reshape((-1,) + (1,) * (len(shape) - 1 - position))
    return factor_of


def noise(own_key, extent, scale, most, split=(), held_as=jnp.bfloat16):
    array = scale * jax.random.normal(own_key, extent, jnp.float32)
    if split:
        array = array * shard_levels(own_key, extent, split, -0.22, 0.18)
    return jnp.clip(array, -most, most).astype(held_as)


def setup_inputs(seed: int = 0) -> dict:
    seeds = jax.random.split(jax.random.key(seed), 5)
    volumes = noise(seeds[0], (VOLUMES, GX, CIN, GRID * GRID), 1.0, 6.0, ((0, 2), (1, 16), (2, 8)))
    kernel = noise(seeds[1], (COUT, 27 * CIN), (27 * CIN // 8) ** -0.5, 0.15625, ((0, 8),))
    bias = noise(seeds[2], (COUT,), 0.5, 3.0, ((0, 8),), jnp.float32)
    act_grad = noise(seeds[3], (VOLUMES, OX, COUT, OG * OG), 1.0, 6.0, ((0, 2), (1, 16), (2, 8)))
    return dict(volumes=volumes, kernel=kernel, bias=bias, act_grad=act_grad)


NUMBERS = ('NDHWC', 'DHWIO', 'NDHWC')

def forward_conv(inputs, filters):
    return lax.conv_general_dilated(inputs, filters, (2, 2, 2), ((1, 1), (1, 1), (1, 1)), dimension_numbers=NUMBERS, preferred_element_type=jnp.float32)

def transpose_conv(grads, flipped):
    return lax.conv_general_dilated(grads, flipped, (1, 1, 1), ((1, 2), (1, 2), (1, 2)), lhs_dilation=(2, 2, 2), dimension_numbers=NUMBERS, preferred_element_type=jnp.float32)

def reference(volumes, kernel, bias, act_grad):
    total_vols = volumes.shape[0]
    vol_cells = volumes.reshape(total_vols, GX, CIN, GRID, GRID).transpose(0, 1, 3, 4, 2)
    filters = kernel.reshape(COUT, 3, 3, 3, CIN).transpose(1, 2, 3, 4, 0)
    grad_cells = act_grad.reshape(total_vols, OX, COUT, OG, OG).transpose(0, 1, 3, 4, 2)
    pre_act = forward_conv(vol_cells, filters) + bias
    activation = jax.nn.gelu(pre_act).astype(jnp.bfloat16)
    _, pull_back = jax.vjp(jax.nn.gelu, pre_act)
    out_grad = pull_back(grad_cells.astype(jnp.float32))[0].astype(jnp.bfloat16)
    group_width = COUT // N_CHAN
    flipped = filters[::-1, ::-1, ::-1].transpose(0, 1, 2, 4, 3)
    total = jnp.zeros(vol_cells.shape, jnp.float32)
    for group in range(N_CHAN):
        lower = group * group_width
        partial_grad = transpose_conv(out_grad[..., lower:lower + group_width], flipped[:, :, :, lower:lower + group_width, :])
        total = total + partial_grad
    grad_cells_x = total.astype(jnp.bfloat16)
    padded = jnp.pad(vol_cells, ((0, 0), (1, 1), (1, 1), (1, 1), (0, 0)))
    out_x, out_y, out_z = (out_grad.shape[1], out_grad.shape[2], out_grad.shape[3])
    flat_grad = out_grad.reshape(-1, COUT)
    tap_terms = []
    for first_tap in range(3):
        for second_tap in range(3):
            for third_tap in range(3):
                window = padded[:, first_tap:first_tap + 2 * out_x:2, second_tap:second_tap + 2 * out_y:2, third_tap:third_tap + 2 * out_z:2, :]
                tap_terms.append(lax.dot_general(window.reshape(-1, CIN), flat_grad, (((0,), (0,)), ((), ())), preferred_element_type=jnp.float32))
    weight_old = jnp.stack(tap_terms).reshape(3, 3, 3, CIN, COUT) / VOLUMES
    grad_b = lax.optimization_barrier(jnp.sum(out_grad.astype(jnp.float32), axis=(0, 1, 2, 3))) / VOLUMES
    activation_out = activation.transpose(0, 1, 4, 2, 3).reshape(total_vols, OX, COUT, OG * OG)
    grad_x = grad_cells_x.transpose(0, 1, 4, 2, 3).reshape(total_vols, GX, CIN, GRID * GRID)
    grad_w = weight_old.transpose(4, 0, 1, 2, 3).reshape(COUT, 27 * CIN)
    return (activation_out, grad_x, grad_w, grad_b)
```

```python
import jax
import jax.numpy as jnp
import numpy as np
from jax import lax
from jax.experimental import pallas as pl
from jax.experimental.pallas import tpu as pltpu
from jax.sharding import PartitionSpec as P

BF = jnp.bfloat16
F32 = jnp.float32
DS = ("dp", "space")
Y_GROUPS = [[dp * 16 + z * 2 + yh for yh in range(2) for dp in range(2)] for z in range(8)]
Z_GROUPS = [[dp * 16 + z * 2 + yh for z in range(8)] for yh in range(2) for dp in range(2)]
X_GROUPS = [[2 * x + core for x in range(4)] for core in range(2)]
TAP_OF = {(0, 0): 1, (1, 0): 2, (1, 1): 0}
PARAMS = pltpu.CompilerParams(vmem_limit_bytes=48 * 1024 * 1024)


def split_matrix():
    matrix = np.zeros((512, 512), np.float32)
    for y in range(16):
        for z in range(32):
            matrix[y * 32 + z, (2 * (y % 2) + z % 2) * 128 + (y // 2) * 16 + z // 2] = 1
    return matrix


def class_shifts(c):
    py, pz = c // 2, c % 2
    return [(sy, sz) for sy in range(py + 1) for sz in range(pz + 1)]


def taps_of(c):
    py, pz = c // 2, c % 2
    return [(TAP_OF[py, sy] * 3 + TAP_OF[pz, sz], sy, sz) for sy, sz in class_shifts(c)]


def lanes(shape):
    return lax.broadcasted_iota(jnp.int32, shape, 1)


def later(a, sy, sz):
    lane = lanes(a.shape)
    if sy:
        a = jnp.where(lane < 16, 0.0, pltpu.roll(a, 16, 1))
    if sz:
        a = jnp.where(lane % 16 == 0, 0.0, pltpu.roll(a, 1, 1))
    return a


def earlier(a, sy, sz):
    lane = lanes(a.shape)
    if sy:
        a = jnp.where(lane >= 240, 0.0, pltpu.roll(a, 240, 1))
    if sz:
        a = jnp.where(lane % 16 == 15, 0.0, pltpu.roll(a, 255, 1))
    return a


def split_kernel(x_ref, m_ref, o_ref):
    for p in range(2):
        for h in range(2):
            r = jnp.dot(x_ref[p, :, h * 512 : (h + 1) * 512], m_ref[...], preferred_element_type=F32).astype(BF)
            for c in range(4):
                for copy in range(4):
                    o_ref[copy, p, c, :, h * 128 : (h + 1) * 128] = r[:, c * 128 : (c + 1) * 128]


def forward_kernel(core_ref, xo_ref, xp_ref, w_ref, xs_ref, own_ref, next_ref):
    core = core_ref[0]
    mine = pl.multiple_of(core * 64, 64)
    other = pl.multiple_of(64 - core * 64, 64)
    for p in range(2):
        for c in range(4):
            for x in range(4):
                xs_ref[p, c, pl.ds(x * 128 + mine, 64), :] = xo_ref[x, p, c]
                xs_ref[p, c, pl.ds(x * 128 + other, 64), :] = xp_ref[x, p, c]
    own = {}
    following = {}

    def add(table, key, value):
        table[key] = table[key] + value if key in table else value

    for c in range(4):
        taps = taps_of(c)
        for p, firsts in ((1, (0, 2)), (0, (1,))):
            rows = []
            for k1 in firsts:
                for tap, _, _ in taps:
                    at = (9 * k1 + tap) * 512
                    rows.append(w_ref[:, at : at + 512])
            r = jnp.dot(jnp.concatenate(rows, 0), xs_ref[p, c], preferred_element_type=F32)
            n = 0
            for k1 in firsts:
                for _, sy, sz in taps:
                    add(following if k1 == 0 else own, (sy, sz), r[64 * n : 64 * n + 64])
                    n += 1
    own_ref[...] = sum(later(v, *s) for s, v in own.items())
    next_ref[...] = sum(later(v, *s) for s, v in following.items())


def gelu_kernel(own_ref, from_ref, b_ref, g_ref, act_ref, dy_ref):
    u = own_ref[...] + from_ref[...] + b_ref[...]
    root = float(np.sqrt(2 / np.pi))
    t = jnp.tanh(root * (u + 0.044715 * (u * u * u)))
    act_ref[...] = (0.5 * u * (1.0 + t)).astype(BF)
    slope = 0.5 * (1.0 + t) + 0.5 * u * (1.0 - t * t) * (root * (1.0 + 3 * 0.044715 * (u * u)))
    dy_ref[...] = (g_ref[...].astype(F32) * slope).astype(BF)


def pair_block(total, shape):
    hi = total.astype(BF).astype(F32)
    lane = lanes(shape)
    return jnp.where(lane == 0, hi, jnp.where(lane == 1, total - hi, 0.0)).astype(BF)


def filter_grad_kernel(dy_ref, dn_ref, xs_ref, o_ref):
    now = dy_ref[...].astype(F32)
    nxt = dn_ref[...].astype(F32)
    shifted = {}
    for sy in range(2):
        for sz in range(2):
            shifted[0, sy, sz] = earlier(nxt, sy, sz).astype(BF)
            shifted[1, sy, sz] = earlier(now, sy, sz).astype(BF)
    for c in range(4):
        taps = taps_of(c)
        for p, firsts in ((0, (1,)), (1, (2, 0))):
            rows = [shifted[min(k1, 1), sy, sz] for k1 in firsts for _, sy, sz in taps]
            r = lax.dot_general(
                jnp.concatenate(rows, 0), xs_ref[p, c], (((1,), (1,)), ((), ())), preferred_element_type=F32
            ).astype(BF)
            n = 0
            for k1 in firsts:
                for tap, _, _ in taps:
                    h, at = divmod(9 * k1 + tap, 14)
                    for q in range(4):
                        for fb in range(4):
                            o_ref[q, fb * 2 + h, :, at * 128 : at * 128 + 128] = r[
                                64 * n + 16 * fb : 64 * n + 16 * fb + 16, q * 128 : q * 128 + 128
                            ]
                    n += 1
    block = pair_block(jnp.sum(now, 1, keepdims=True), (64, 128))
    for q in range(4):
        for fb in range(4):
            o_ref[q, fb * 2 + 1, :, 13 * 128 : 14 * 128] = block[16 * fb : 16 * fb + 16]


def sum_y_kernel(r_ref, o_ref):
    for z in range(8):
        for at in range(0, 1792, 256):
            total = sum(r_ref[s, z, :, at : at + 256].astype(F32) for s in range(4))
            o_ref[z, :, at : at + 256] = total.astype(BF)
            if z % 2 == 1 and at == 1536:
                bias_total = total[:, 128:129] + total[:, 129:130]
                o_ref[z, :, 1664:1792] = pair_block(bias_total, (16, 128))


def sum_z_kernel(odd_ref, r_ref, o_ref):
    for at in range(0, 1792, 256):
        total = sum(r_ref[s, :, at : at + 256].astype(F32) for s in range(8))
        out = total.astype(BF)
        for copy in range(8):
            o_ref[copy, :, at : at + 256] = out
        if at == 1536:

            @pl.when(odd_ref[0] == 1)
            def _():
                bias_total = total[:, 128:129] + total[:, 129:130]
                block = pair_block(bias_total, (16, 128))
                for copy in range(8):
                    o_ref[copy, :, 1664:1792] = block


def filter_out_kernel(r_ref, w_ref, b_ref):
    for tap in range(27):
        h, at = divmod(tap, 14)
        for q in range(4):
            for fb in range(4):
                w_ref[fb * 16 : fb * 16 + 16, tap * 512 + q * 128 : tap * 512 + q * 128 + 128] = (
                    r_ref[q, fb * 2 + h, :, at * 128 : at * 128 + 128].astype(F32) * 0.5
                )
    for fb in range(4):
        pair = r_ref[0, fb * 2 + 1, :, 1664:1792].astype(F32)
        b_ref[fb * 16 : fb * 16 + 16, :] = (pair[:, 0:1] + pair[:, 1:2]) * 0.5


def pack_kernel(x_ref, w_ref, *o_refs):
    for d in range(4):
        to = lax.rem(x_ref[0] + d, 4) * 128
        for tap in range(27):
            o_refs[d][:, tap * 128 : tap * 128 + 128] = w_ref[:, pl.ds(pl.multiple_of(tap * 512 + to, 128), 128)]


def input_grad_kernel(core_ref, *refs):
    w_refs, d_refs, (mine_ref, theirs_ref), (g_ref,) = refs[:4], refs[4:8], refs[8:10], refs[10:]
    shifted = {}
    for which in range(2):
        full = jnp.concatenate([d[which] for d in d_refs], 0).astype(F32)
        for sy in range(2):
            for sz in range(2):
                shifted[which, sy, sz] = earlier(full, sy, sz).astype(BF)
    mine = pl.multiple_of(core_ref[0] * 64, 64)
    other = pl.multiple_of(64 - core_ref[0] * 64, 64)
    for c in range(4):
        for p, firsts in ((0, (1,)), (1, (2, 0))):
            total = None
            for k1 in firsts:
                for tap, sy, sz in taps_of(c):
                    at = (9 * k1 + tap) * 128
                    w = jnp.concatenate([w[:, at : at + 128] for w in w_refs], 0)
                    r = lax.dot_general(
                        w, shifted[1 if k1 == 0 else 0, sy, sz], (((0,), (0,)), ((), ())), preferred_element_type=F32
                    )
                    total = r if total is None else total + r
            g_ref[...] = total
            mine_ref[p, c] = g_ref[pl.ds(mine, 64), :]
            theirs_ref[p, c] = g_ref[pl.ds(other, 64), :]


def join_kernel(a_ref, b_ref, m_ref, o_ref):
    for p in range(2):
        for h in range(2):
            at = slice(h * 128, h * 128 + 128)
            parts = [(a_ref[p, c, :, at] + b_ref[p, c, :, at]).astype(BF) for c in range(4)]
            r = lax.dot_general(
                jnp.concatenate(parts, 1), m_ref[...], (((1,), (1,)), ((), ())), preferred_element_type=F32
            )
            o_ref[p, :, h * 512 : (h + 1) * 512] = r.astype(BF)


VMEM = pl.BlockSpec(memory_space=pltpu.VMEM)
SMEM = pl.BlockSpec(memory_space=pltpu.SMEM)


def call(kernel, outs, *args, scalars=0, scratch=()):
    shapes = [jax.ShapeDtypeStruct(s, t) for s, t in outs]
    result = pl.pallas_call(
        kernel,
        out_shape=shapes,
        in_specs=[SMEM] * scalars + [VMEM] * (len(args) - scalars),
        out_specs=[VMEM] * len(outs),
        scratch_shapes=list(scratch),
        compiler_params=PARAMS,
    )(*args)
    return result


def shift_space(a, by):
    return lax.ppermute(a, "space", [(i, i + by) for i in range(16) if 0 <= i + by < 16])


def to_x(a, d):
    return lax.ppermute(a, "chan", [(i, (i + 2 * d) % 8) for i in range(8)])


def to_partner(a):
    return lax.ppermute(a, "chan", [(i, i ^ 1) for i in range(8)])


def per_device(volumes, kernel, bias, act_grad):
    chan = lax.axis_index("chan")
    core = (chan % 2).astype(jnp.int32).reshape(1)
    x = (chan // 2).astype(jnp.int32).reshape(1)
    z_odd = ((lax.axis_index("space") // 2) % 2).astype(jnp.int32).reshape(1)
    matrix = jnp.asarray(split_matrix(), BF)

    (copies,) = call(split_kernel, [((4, 2, 4, 64, 256), BF)], volumes.reshape(2, 64, 1024), matrix)
    x_own = lax.all_to_all(copies, "chan", 0, 0, axis_index_groups=X_GROUPS)
    x_partner = to_partner(x_own)
    xs, own, following = call(
        forward_kernel,
        [((2, 4, 512, 256), BF), ((64, 256), F32), ((64, 256), F32)],
        core,
        x_own,
        x_partner,
        kernel,
        scalars=1,
    )
    received = shift_space(following, 1)
    packed = call(pack_kernel, [((64, 3456), BF)] * 4, x, kernel, scalars=1)
    *packed, received = lax.optimization_barrier((*packed, received))
    weights = [packed[0]] + [to_x(packed[d], d) for d in range(1, 4)]
    activation, dy = call(
        gelu_kernel,
        [((64, 256), BF), ((64, 256), BF)],
        own,
        received,
        bias.reshape(64, 1),
        act_grad.reshape(64, 256),
    )
    dy_next = shift_space(dy, -1)
    (terms,) = call(filter_grad_kernel, [((4, 8, 16, 1792), BF)], dy, dy_next, xs)
    dys = jnp.stack([dy, dy_next])
    grads = [dys] + [to_x(dys, d) for d in range(1, 4)]

    terms = lax.all_to_all(terms, DS, 0, 0, axis_index_groups=Y_GROUPS)
    (terms,) = call(sum_y_kernel, [((8, 16, 1792), BF)], terms)
    terms = lax.all_to_all(terms, DS, 0, 0, axis_index_groups=Z_GROUPS)
    (terms,) = call(sum_z_kernel, [((8, 16, 1792), BF)], z_odd, terms, scalars=1)
    terms = lax.all_to_all(terms, DS, 0, 0, axis_index_groups=Z_GROUPS)
    terms = lax.all_to_all(jnp.broadcast_to(terms[None], (4, 8, 16, 1792)), DS, 0, 0, axis_index_groups=Y_GROUPS)
    grad_w, grad_b = call(filter_out_kernel, [((64, 13824), F32), ((64, 1), F32)], terms)

    mine, theirs = call(
        input_grad_kernel,
        [((2, 4, 64, 256), F32), ((2, 4, 64, 256), F32)],
        core,
        *weights,
        *grads,
        scalars=1,
        scratch=[pltpu.VMEM((128, 256), F32)],
    )
    (grad_x,) = call(join_kernel, [((2, 64, 1024), BF)], mine, to_partner(theirs), matrix)
    return (
        activation.reshape(1, 1, 64, 256),
        grad_x.reshape(1, 2, 64, 1024),
        grad_w,
        grad_b.reshape(64),
    )


def solution(mesh):
    in_specs = (
        P("dp", "space", "chan", None),
        P("chan", None),
        P("chan"),
        P("dp", "space", "chan", None),
    )
    out_specs = (
        P("dp", "space", "chan", None),
        P("dp", "space", "chan", None),
        P("chan", None),
        P("chan"),
    )
    return jax.shard_map(
        per_device, mesh=mesh, in_specs=in_specs, out_specs=out_specs, check_vma=False
    )
```

```python
import jax
import jax.numpy as jnp
import numpy as np
from jax import lax
from jax.experimental import pallas as pl
from jax.experimental.pallas import tpu as pltpu
from jax.sharding import PartitionSpec as P

BF = jnp.bfloat16
F32 = jnp.float32
DS = ("dp", "space")
Y_GROUPS = [[dp * 16 + z * 2 + yh for yh in range(2) for dp in range(2)] for z in range(8)]
Z_GROUPS = [[dp * 16 + z * 2 + yh for z in range(8)] for yh in range(2) for dp in range(2)]
X_GROUPS = [[2 * x + core for x in range(4)] for core in range(2)]
TAP_OF = {(0, 0): 1, (1, 0): 2, (1, 1): 0}
PARAMS = pltpu.CompilerParams(vmem_limit_bytes=48 * 1024 * 1024)


def split_matrix():
    matrix = np.zeros((512, 512), np.float32)
    for y in range(16):
        for z in range(32):
            matrix[y * 32 + z, (2 * (y % 2) + z % 2) * 128 + (y // 2) * 16 + z // 2] = 1
    return matrix


def class_shifts(c):
    py, pz = c // 2, c % 2
    return [(sy, sz) for sy in range(py + 1) for sz in range(pz + 1)]


def taps_of(c):
    py, pz = c // 2, c % 2
    return [(TAP_OF[py, sy] * 3 + TAP_OF[pz, sz], sy, sz) for sy, sz in class_shifts(c)]


def lanes(shape):
    return lax.broadcasted_iota(jnp.int32, shape, 1)


def later(a, sy, sz):
    lane = lanes(a.shape)
    if sy:
        a = jnp.where(lane < 16, 0.0, pltpu.roll(a, 16, 1))
    if sz:
        a = jnp.where(lane % 16 == 0, 0.0, pltpu.roll(a, 1, 1))
    return a


def earlier(a, sy, sz):
    lane = lanes(a.shape)
    width = a.shape[1]
    if sy:
        a = jnp.where(lane % 256 >= 240, 0.0, pltpu.roll(a, width - 16, 1))
    if sz:
        a = jnp.where(lane % 16 == 15, 0.0, pltpu.roll(a, width - 1, 1))
    return a


def split_kernel(x_ref, m_ref, o_ref):
    for p in range(2):
        for h in range(2):
            r = jnp.dot(x_ref[p, :, h * 512 : (h + 1) * 512], m_ref[...], preferred_element_type=F32).astype(BF)
            for c in range(4):
                for copy in range(4):
                    o_ref[copy, p, c, :, h * 128 : (h + 1) * 128] = r[:, c * 128 : (c + 1) * 128]


def forward_kernel(core_ref, xo_ref, xp_ref, w_ref, own_ref, next_ref, xs_ref):
    core = core_ref[0]
    mine = pl.multiple_of(core * 64, 64)
    other = pl.multiple_of(64 - core * 64, 64)
    for p in range(2):
        for c in range(4):
            for x in range(4):
                xs_ref[p, c, pl.ds(x * 128 + mine, 64), :] = xo_ref[x, p, c]
                xs_ref[p, c, pl.ds(x * 128 + other, 64), :] = xp_ref[x, p, c]
    own = {}
    following = {}

    def add(table, key, value):
        table[key] = table[key] + value if key in table else value

    for c in range(4):
        taps = taps_of(c)
        for p, firsts in ((1, (0, 2)), (0, (1,))):
            rows = []
            for k1 in firsts:
                for tap, _, _ in taps:
                    at = (9 * k1 + tap) * 512
                    rows.append(w_ref[:, at : at + 512])
            r = jnp.dot(jnp.concatenate(rows, 0), xs_ref[p, c], preferred_element_type=F32)
            n = 0
            for k1 in firsts:
                for _, sy, sz in taps:
                    add(following if k1 == 0 else own, (sy, sz), r[64 * n : 64 * n + 64])
                    n += 1
    own_ref[...] = sum(later(v, *s) for s, v in own.items())
    next_ref[...] = sum(later(v, *s) for s, v in following.items())


def gelu_kernel(own_ref, from_ref, b_ref, g_ref, act_ref, dy_ref):
    u = own_ref[...] + from_ref[...] + b_ref[...]
    root = float(np.sqrt(2 / np.pi))
    t = jnp.tanh(root * (u + 0.044715 * (u * u * u)))
    act_ref[...] = (0.5 * u * (1.0 + t)).astype(BF)
    slope = 0.5 * (1.0 + t) + 0.5 * u * (1.0 - t * t) * (root * (1.0 + 3 * 0.044715 * (u * u)))
    dy = (g_ref[...].astype(F32) * slope).astype(BF)
    for copy in range(4):
        dy_ref[copy] = dy


def pair_block(total, shape):
    hi = total.astype(BF).astype(F32)
    lane = lanes(shape)
    return jnp.where(lane == 0, hi, jnp.where(lane == 1, total - hi, 0.0)).astype(BF)


def filter_grad_kernel(where_ref, dy_ref, dn_ref, xo_ref, xp_ref, o_ref, both_ref, xs_ref):
    mine = pl.multiple_of(where_ref[0] * 64, 64)
    other = pl.multiple_of(64 - where_ref[0] * 64, 64)
    for c in range(4):
        for p in range(2):
            for y in range(4):
                xs_ref[c, pl.ds(p * 128 + mine, 64), y * 256 : y * 256 + 256] = xo_ref[y, p, c]
                xs_ref[c, pl.ds(p * 128 + other, 64), y * 256 : y * 256 + 256] = xp_ref[y, p, c]
    q = where_ref[1]
    both_ref[0] = dy_ref[q]

    @pl.when(q < 2)
    def _():
        both_ref[1] = dy_ref[lax.rem(q + 2, 4)]

    @pl.when(q >= 2)
    def _():
        both_ref[1] = dn_ref[lax.rem(q, 2)]

    now = jnp.concatenate([dy_ref[y] for y in range(4)], 1).astype(F32)
    nxt = jnp.concatenate([dy_ref[2], dy_ref[3], dn_ref[0], dn_ref[1]], 1).astype(F32)
    for c in range(4):
        taps = taps_of(c)
        for grads, firsts, rows in ((now, (1, 2), slice(0, 256)), (nxt, (0,), slice(128, 256))):
            left = jnp.concatenate([earlier(grads, sy, sz).astype(BF) for _, sy, sz in taps], 0)
            r = lax.dot_general(
                left, xs_ref[c, rows, :], (((1,), (1,)), ((), ())), preferred_element_type=F32
            ).astype(BF)
            for n, (tap, _, _) in enumerate(taps):
                for m, k1 in enumerate(firsts):
                    h, at = divmod(9 * k1 + tap, 14)
                    for fb in range(4):
                        o_ref[fb * 2 + h, :, at * 128 : at * 128 + 128] = r[
                            64 * n + 16 * fb : 64 * n + 16 * fb + 16, m * 128 : m * 128 + 128
                        ]
    block = pair_block(jnp.sum(now, 1, keepdims=True), (64, 128))
    for fb in range(4):
        o_ref[fb * 2 + 1, :, 13 * 128 : 14 * 128] = block[16 * fb : 16 * fb + 16]


def sum_z_kernel(odd_ref, r_ref, o_ref):
    for at in range(0, 1792, 256):
        total = sum(r_ref[s, :, at : at + 256].astype(F32) for s in range(8))
        out = total.astype(BF)
        for copy in range(8):
            o_ref[copy, :, at : at + 256] = out
        if at == 1536:

            @pl.when(odd_ref[0] == 1)
            def _():
                bias_total = total[:, 128:129] + total[:, 129:130]
                block = pair_block(bias_total, (16, 128))
                for copy in range(8):
                    o_ref[copy, :, 1664:1792] = block


def filter_out_kernel(r_ref, w_ref, b_ref):
    for tap in range(27):
        h, at = divmod(tap, 14)
        for q in range(4):
            for fb in range(4):
                w_ref[fb * 16 : fb * 16 + 16, tap * 512 + q * 128 : tap * 512 + q * 128 + 128] = (
                    r_ref[q, fb * 2 + h, :, at * 128 : at * 128 + 128].astype(F32) * 0.5
                )
    for fb in range(4):
        pair = r_ref[0, fb * 2 + 1, :, 1664:1792].astype(F32)
        b_ref[fb * 16 : fb * 16 + 16, :] = (pair[:, 0:1] + pair[:, 1:2]) * 0.5


def pack_kernel(x_ref, w_ref, *o_refs):
    for d in range(4):
        to = lax.rem(x_ref[0] + d, 4) * 128
        for tap in range(27):
            o_refs[d][:, tap * 128 : tap * 128 + 128] = w_ref[:, pl.ds(pl.multiple_of(tap * 512 + to, 128), 128)]


def input_grad_kernel(core_ref, *refs):
    w_refs, d_refs, (mine_ref, theirs_ref), (g_ref,) = refs[:4], refs[4:8], refs[8:10], refs[10:]
    shifted = {}
    for which in range(2):
        full = jnp.concatenate([d[which] for d in d_refs], 0).astype(F32)
        for sy in range(2):
            for sz in range(2):
                shifted[which, sy, sz] = earlier(full, sy, sz).astype(BF)
    mine = pl.multiple_of(core_ref[0] * 64, 64)
    other = pl.multiple_of(64 - core_ref[0] * 64, 64)
    for c in range(4):
        for p, firsts in ((0, (1,)), (1, (2, 0))):
            total = None
            for k1 in firsts:
                for tap, sy, sz in taps_of(c):
                    at = (9 * k1 + tap) * 128
                    w = jnp.concatenate([w[:, at : at + 128] for w in w_refs], 0)
                    r = lax.dot_general(
                        w, shifted[1 if k1 == 0 else 0, sy, sz], (((0,), (0,)), ((), ())), preferred_element_type=F32
                    )
                    total = r if total is None else total + r
            g_ref[...] = total
            mine_ref[p, c] = g_ref[pl.ds(mine, 64), :]
            theirs_ref[p, c] = g_ref[pl.ds(other, 64), :]


def join_kernel(a_ref, b_ref, m_ref, o_ref):
    for p in range(2):
        for h in range(2):
            at = slice(h * 128, h * 128 + 128)
            parts = [(a_ref[p, c, :, at] + b_ref[p, c, :, at]).astype(BF) for c in range(4)]
            r = lax.dot_general(
                jnp.concatenate(parts, 1), m_ref[...], (((1,), (1,)), ((), ())), preferred_element_type=F32
            )
            o_ref[p, :, h * 512 : (h + 1) * 512] = r.astype(BF)


VMEM = pl.BlockSpec(memory_space=pltpu.VMEM)
SMEM = pl.BlockSpec(memory_space=pltpu.SMEM)


def call(kernel, outs, *args, scalars=0, scratch=()):
    shapes = [jax.ShapeDtypeStruct(s, t) for s, t in outs]
    result = pl.pallas_call(
        kernel,
        out_shape=shapes,
        in_specs=[SMEM] * scalars + [VMEM] * (len(args) - scalars),
        out_specs=[VMEM] * len(outs),
        scratch_shapes=list(scratch),
        compiler_params=PARAMS,
    )(*args)
    return result


def shift_space(a, by):
    return lax.ppermute(a, "space", [(i, i + by) for i in range(16) if 0 <= i + by < 16])


def to_x(a, d):
    return lax.ppermute(a, "chan", [(i, (i + 2 * d) % 8) for i in range(8)])


def to_partner(a):
    return lax.ppermute(a, "chan", [(i, i ^ 1) for i in range(8)])


def per_device(volumes, kernel, bias, act_grad):
    chan = lax.axis_index("chan")
    core = (chan % 2).astype(jnp.int32).reshape(1)
    x = (chan // 2).astype(jnp.int32).reshape(1)
    z_odd = ((lax.axis_index("space") // 2) % 2).astype(jnp.int32).reshape(1)
    matrix = jnp.asarray(split_matrix(), BF)

    q = ((lax.axis_index("space") % 2) * 2 + lax.axis_index("dp")).astype(jnp.int32)
    where = jnp.stack([core[0], q])

    (copies,) = call(split_kernel, [((4, 2, 4, 64, 256), BF)], volumes.reshape(2, 64, 1024), matrix)
    x_own = lax.all_to_all(copies, "chan", 0, 0, axis_index_groups=X_GROUPS)
    x_partner = to_partner(x_own)
    ring_own = lax.all_to_all(x_own, DS, 0, 0, axis_index_groups=Y_GROUPS)
    ring_partner = to_partner(ring_own)
    own, following = call(
        forward_kernel,
        [((64, 256), F32), ((64, 256), F32)],
        core,
        x_own,
        x_partner,
        kernel,
        scalars=1,
        scratch=[pltpu.VMEM((2, 4, 512, 256), BF)],
    )
    received = shift_space(following, 1)
    packed = call(pack_kernel, [((64, 3456), BF)] * 4, x, kernel, scalars=1)
    *packed, received = lax.optimization_barrier((*packed, received))
    weights = [packed[0]] + [to_x(packed[d], d) for d in range(1, 4)]
    activation, dy_copies = call(
        gelu_kernel,
        [((64, 256), BF), ((4, 64, 256), BF)],
        own,
        received,
        bias.reshape(64, 1),
        act_grad.reshape(64, 256),
    )
    dy = lax.all_to_all(dy_copies, DS, 0, 0, axis_index_groups=Y_GROUPS)
    dy_next = shift_space(dy[:2], -2)
    terms, both = call(
        filter_grad_kernel,
        [((8, 16, 1792), BF), ((2, 64, 256), BF)],
        where,
        dy,
        dy_next,
        ring_own,
        ring_partner,
        scalars=1,
        scratch=[pltpu.VMEM((4, 256, 1024), BF)],
    )
    grads = [both] + [to_x(both, d) for d in range(1, 4)]

    terms = lax.all_to_all(terms, DS, 0, 0, axis_index_groups=Z_GROUPS)
    *inputs, terms = lax.optimization_barrier((*weights, *grads, terms))
    (terms,) = call(sum_z_kernel, [((8, 16, 1792), BF)], z_odd, terms, scalars=1)
    mine, theirs = call(
        input_grad_kernel,
        [((2, 4, 64, 256), F32), ((2, 4, 64, 256), F32)],
        core,
        *inputs,
        scalars=1,
        scratch=[pltpu.VMEM((128, 256), F32)],
    )
    terms = lax.all_to_all(terms, DS, 0, 0, axis_index_groups=Z_GROUPS)
    theirs = to_partner(theirs)
    mine, theirs, terms = lax.optimization_barrier((mine, theirs, terms))
    terms = lax.all_to_all(jnp.broadcast_to(terms[None], (4, 8, 16, 1792)), DS, 0, 0, axis_index_groups=Y_GROUPS)
    grad_w, grad_b = call(filter_out_kernel, [((64, 13824), F32), ((64, 1), F32)], terms)
    (grad_x,) = call(join_kernel, [((2, 64, 1024), BF)], mine, theirs, matrix)
    return (
        activation.reshape(1, 1, 64, 256),
        grad_x.reshape(1, 2, 64, 1024),
        grad_w,
        grad_b.reshape(64),
    )


def solution(mesh):
    in_specs = (
        P("dp", "space", "chan", None),
        P("chan", None),
        P("chan"),
        P("dp", "space", "chan", None),
    )
    out_specs = (
        P("dp", "space", "chan", None),
        P("dp", "space", "chan", None),
        P("chan", None),
        P("chan"),
    )
    return jax.shard_map(
        per_device, mesh=mesh, in_specs=in_specs, out_specs=out_specs, check_vma=False
    )
```

```python
import jax
import jax.numpy as jnp
import numpy as np
from jax import lax
from jax.experimental import pallas as pl
from jax.experimental.pallas import tpu as pltpu
from jax.sharding import PartitionSpec as P

BF = jnp.bfloat16
F32 = jnp.float32
DS = ("dp", "space")
Y_GROUPS = [[dp * 16 + z * 2 + yh for yh in range(2) for dp in range(2)] for z in range(8)]
Z_GROUPS = [[dp * 16 + z * 2 + yh for z in range(8)] for yh in range(2) for dp in range(2)]
X_GROUPS = [[2 * x + core for x in range(4)] for core in range(2)]
TAP_OF = {(0, 0): 1, (1, 0): 2, (1, 1): 0}
PARAMS = pltpu.CompilerParams(vmem_limit_bytes=48 * 1024 * 1024)


def split_matrix():
    matrix = np.zeros((512, 512), np.float32)
    for y in range(16):
        for z in range(32):
            matrix[y * 32 + z, (2 * (y % 2) + z % 2) * 128 + (y // 2) * 16 + z // 2] = 1
    return matrix


def class_shifts(c):
    py, pz = c // 2, c % 2
    return [(sy, sz) for sy in range(py + 1) for sz in range(pz + 1)]


def taps_of(c):
    py, pz = c // 2, c % 2
    return [(TAP_OF[py, sy] * 3 + TAP_OF[pz, sz], sy, sz) for sy, sz in class_shifts(c)]


def lanes(shape):
    return lax.broadcasted_iota(jnp.int32, shape, 1)


def later(a, sy, sz):
    lane = lanes(a.shape)
    if sy:
        a = jnp.where(lane < 16, 0.0, pltpu.roll(a, 16, 1))
    if sz:
        a = jnp.where(lane % 16 == 0, 0.0, pltpu.roll(a, 1, 1))
    return a


def earlier(a, sy, sz):
    lane = lanes(a.shape)
    width = a.shape[1]
    if sy:
        a = jnp.where(lane % 256 >= 240, 0.0, pltpu.roll(a, width - 16, 1))
    if sz:
        a = jnp.where(lane % 16 == 15, 0.0, pltpu.roll(a, width - 1, 1))
    return a


def split_kernel(x_ref, m_ref, o_ref):
    for p in range(2):
        for h in range(2):
            r = jnp.dot(x_ref[p, :, h * 512 : (h + 1) * 512], m_ref[...], preferred_element_type=F32).astype(BF)
            for c in range(4):
                for copy in range(4):
                    o_ref[copy, p, c, :, h * 128 : (h + 1) * 128] = r[:, c * 128 : (c + 1) * 128]


def forward_kernel(core_ref, xo_ref, xp_ref, w_ref, own_ref, next_ref, xs_ref):
    core = core_ref[0]
    mine = pl.multiple_of(core * 64, 64)
    other = pl.multiple_of(64 - core * 64, 64)
    for p in range(2):
        for c in range(4):
            for x in range(4):
                xs_ref[p, c, pl.ds(x * 128 + mine, 64), :] = xo_ref[x, p, c]
                xs_ref[p, c, pl.ds(x * 128 + other, 64), :] = xp_ref[x, p, c]
    own = {}
    following = {}

    def add(table, key, value):
        table[key] = table[key] + value if key in table else value

    for c in range(4):
        taps = taps_of(c)
        for p, firsts in ((1, (0, 2)), (0, (1,))):
            rows = []
            for k1 in firsts:
                for tap, _, _ in taps:
                    at = (9 * k1 + tap) * 512
                    rows.append(w_ref[:, at : at + 512])
            r = jnp.dot(jnp.concatenate(rows, 0), xs_ref[p, c], preferred_element_type=F32)
            n = 0
            for k1 in firsts:
                for _, sy, sz in taps:
                    add(following if k1 == 0 else own, (sy, sz), r[64 * n : 64 * n + 64])
                    n += 1
    own_ref[...] = sum(later(v, *s) for s, v in own.items())
    next_ref[...] = sum(later(v, *s) for s, v in following.items())


def gelu_kernel(own_ref, from_ref, b_ref, g_ref, act_ref, dy_ref):
    u = own_ref[...] + from_ref[...] + b_ref[...]
    root = float(np.sqrt(2 / np.pi))
    t = jnp.tanh(root * (u + 0.044715 * (u * u * u)))
    act_ref[...] = (0.5 * u * (1.0 + t)).astype(BF)
    slope = 0.5 * (1.0 + t) + 0.5 * u * (1.0 - t * t) * (root * (1.0 + 3 * 0.044715 * (u * u)))
    dy = (g_ref[...].astype(F32) * slope).astype(BF)
    for copy in range(4):
        dy_ref[copy] = dy


def pair_block(total, shape):
    hi = total.astype(BF).astype(F32)
    lane = lanes(shape)
    return jnp.where(lane == 0, hi, jnp.where(lane == 1, total - hi, 0.0)).astype(BF)


def filter_grad_kernel(core_ref, dy_ref, xo_ref, xp_ref, e_ref, o_ref, xs_ref):
    mine = pl.multiple_of(core_ref[0] * 64, 64)
    other = pl.multiple_of(64 - core_ref[0] * 64, 64)
    for at, x_ref, side in ((mine, xo_ref, 0), (other, xp_ref, 1)):
        for c in range(4):
            for y in range(4):
                cells = slice(y * 256, y * 256 + 256)
                xs_ref[c, pl.ds(at, 64), cells] = e_ref[side, y, c] if y < 2 else x_ref[y - 2, 1, c]
                xs_ref[c, pl.ds(128 + at, 64), cells] = x_ref[y, 0, c]
                xs_ref[c, pl.ds(256 + at, 64), cells] = x_ref[y, 1, c]
    grads = jnp.concatenate([dy_ref[y] for y in range(4)], 1).astype(F32)
    shifted = {(sy, sz): earlier(grads, sy, sz).astype(BF) for sy in range(2) for sz in range(2)}
    for c in range(4):
        taps = taps_of(c)
        r = lax.dot_general(
            jnp.concatenate([shifted[sy, sz] for _, sy, sz in taps], 0),
            xs_ref[c],
            (((1,), (1,)), ((), ())),
            preferred_element_type=F32,
        ).astype(BF)
        for n, (tap, _, _) in enumerate(taps):
            for k1 in range(3):
                h, at = divmod(9 * k1 + tap, 14)
                for fb in range(4):
                    o_ref[fb * 2 + h, :, at * 128 : at * 128 + 128] = r[
                        64 * n + 16 * fb : 64 * n + 16 * fb + 16, k1 * 128 : k1 * 128 + 128
                    ]
    block = pair_block(jnp.sum(grads, 1, keepdims=True), (64, 128))
    for fb in range(4):
        o_ref[fb * 2 + 1, :, 13 * 128 : 14 * 128] = block[16 * fb : 16 * fb + 16]


def sum_z_kernel(odd_ref, r_ref, o_ref):
    for at in range(0, 1792, 256):
        total = sum(r_ref[s, :, at : at + 256].astype(F32) for s in range(8))
        out = total.astype(BF)
        for copy in range(8):
            o_ref[copy, :, at : at + 256] = out
        if at == 1536:

            @pl.when(odd_ref[0] == 1)
            def _():
                bias_total = total[:, 128:129] + total[:, 129:130]
                block = pair_block(bias_total, (16, 128))
                for copy in range(8):
                    o_ref[copy, :, 1664:1792] = block


def filter_out_kernel(r_ref, w_ref, b_ref):
    for tap in range(27):
        h, at = divmod(tap, 14)
        for q in range(4):
            for fb in range(4):
                w_ref[fb * 16 : fb * 16 + 16, tap * 512 + q * 128 : tap * 512 + q * 128 + 128] = (
                    r_ref[q, fb * 2 + h, :, at * 128 : at * 128 + 128].astype(F32) * 0.5
                )
    for fb in range(4):
        pair = r_ref[0, fb * 2 + 1, :, 1664:1792].astype(F32)
        b_ref[fb * 16 : fb * 16 + 16, :] = (pair[:, 0:1] + pair[:, 1:2]) * 0.5


def pack_kernel(x_ref, w_ref, *o_refs):
    for d in range(4):
        to = lax.rem(x_ref[0] + d, 4) * 128
        for tap in range(27):
            o_refs[d][:, tap * 128 : tap * 128 + 128] = w_ref[:, pl.ds(pl.multiple_of(tap * 512 + to, 128), 128)]


def input_grad_kernel(core_ref, *refs):
    w_refs, d_refs, (mine_ref, theirs_ref), (g_ref,) = refs[:4], refs[4:8], refs[8:10], refs[10:]
    shifted = {}
    for which in range(2):
        full = jnp.concatenate([d[which] for d in d_refs], 0).astype(F32)
        for sy in range(2):
            for sz in range(2):
                shifted[which, sy, sz] = earlier(full, sy, sz).astype(BF)
    mine = pl.multiple_of(core_ref[0] * 64, 64)
    other = pl.multiple_of(64 - core_ref[0] * 64, 64)
    for c in range(4):
        for p, firsts in ((0, (1,)), (1, (2, 0))):
            total = None
            for k1 in firsts:
                for tap, sy, sz in taps_of(c):
                    at = (9 * k1 + tap) * 128
                    w = jnp.concatenate([w[:, at : at + 128] for w in w_refs], 0)
                    r = lax.dot_general(
                        w, shifted[1 if k1 == 0 else 0, sy, sz], (((0,), (0,)), ((), ())), preferred_element_type=F32
                    )
                    total = r if total is None else total + r
            g_ref[...] = total
            mine_ref[p, c] = g_ref[pl.ds(mine, 64), :]
            theirs_ref[p, c] = g_ref[pl.ds(other, 64), :]


def edge_kernel(o_in, p_in, o_ref):
    o_ref[0] = o_in[...]
    o_ref[1] = p_in[...]


def join_kernel(a_ref, b_ref, m_ref, o_ref):
    for p in range(2):
        for h in range(2):
            at = slice(h * 128, h * 128 + 128)
            parts = [(a_ref[p, c, :, at] + b_ref[p, c, :, at]).astype(BF) for c in range(4)]
            r = lax.dot_general(
                jnp.concatenate(parts, 1), m_ref[...], (((1,), (1,)), ((), ())), preferred_element_type=F32
            )
            o_ref[p, :, h * 512 : (h + 1) * 512] = r.astype(BF)


VMEM = pl.BlockSpec(memory_space=pltpu.VMEM)
SMEM = pl.BlockSpec(memory_space=pltpu.SMEM)


def call(kernel, outs, *args, scalars=0, scratch=()):
    shapes = [jax.ShapeDtypeStruct(s, t) for s, t in outs]
    result = pl.pallas_call(
        kernel,
        out_shape=shapes,
        in_specs=[SMEM] * scalars + [VMEM] * (len(args) - scalars),
        out_specs=[VMEM] * len(outs),
        scratch_shapes=list(scratch),
        compiler_params=PARAMS,
    )(*args)
    return result


def shift_space(a, by):
    return lax.ppermute(a, "space", [(i, i + by) for i in range(16) if 0 <= i + by < 16])


def to_x(a, d):
    return lax.ppermute(a, "chan", [(i, (i + 2 * d) % 8) for i in range(8)])


def to_partner(a):
    return lax.ppermute(a, "chan", [(i, i ^ 1) for i in range(8)])


def per_device(volumes, kernel, bias, act_grad):
    chan = lax.axis_index("chan")
    core = (chan % 2).astype(jnp.int32).reshape(1)
    x = (chan // 2).astype(jnp.int32).reshape(1)
    z_odd = ((lax.axis_index("space") // 2) % 2).astype(jnp.int32).reshape(1)
    matrix = jnp.asarray(split_matrix(), BF)

    (copies,) = call(split_kernel, [((4, 2, 4, 64, 256), BF)], volumes.reshape(2, 64, 1024), matrix)
    x_own = lax.all_to_all(copies, "chan", 0, 0, axis_index_groups=X_GROUPS)
    packed = call(pack_kernel, [((64, 3456), BF)] * 4, x, kernel, scalars=1)
    *packed, x_own = lax.optimization_barrier((*packed, x_own))
    ring_own = lax.all_to_all(x_own, DS, 0, 0, axis_index_groups=Y_GROUPS)
    x_partner = to_partner(x_own)
    near = [to_x(packed[1], 1), to_x(packed[3], 3)]
    own, following = call(
        forward_kernel,
        [((64, 256), F32), ((64, 256), F32)],
        core,
        x_own,
        x_partner,
        kernel,
        scalars=1,
        scratch=[pltpu.VMEM((2, 4, 512, 256), BF)],
    )
    received = shift_space(following, 1)
    ring_own, _, *near = lax.optimization_barrier((ring_own, received, *near))
    far = to_x(packed[2], 2)
    ring_partner = to_partner(ring_own)
    activation, dy_copies = call(
        gelu_kernel,
        [((64, 256), BF), ((4, 64, 256), BF)],
        own,
        received,
        bias.reshape(64, 1),
        act_grad.reshape(64, 256),
    )
    piece = pl.BlockSpec((2, None, 4, 64, 256), lambda i: (1, 1, 0, 0, 0))
    edge = pl.pallas_call(
        edge_kernel,
        grid=(1,),
        out_shape=jax.ShapeDtypeStruct((2, 2, 4, 64, 256), BF),
        in_specs=[piece, piece],
        out_specs=pl.BlockSpec((2, 2, 4, 64, 256), lambda i: (0, 0, 0, 0, 0)),
        compiler_params=PARAMS,
    )(ring_own, ring_partner)
    edge = shift_space(edge, 2)
    dy = lax.all_to_all(dy_copies, DS, 0, 0, axis_index_groups=Y_GROUPS)
    dy_next = shift_space(dy_copies[0], -1)
    (terms,) = call(
        filter_grad_kernel,
        [((8, 16, 1792), BF)],
        core,
        dy,
        ring_own,
        ring_partner,
        edge,
        scalars=1,
        scratch=[pltpu.VMEM((4, 384, 1024), BF)],
    )
    terms, far, dy_next = lax.optimization_barrier((terms, far, dy_next))
    terms = lax.all_to_all(terms, DS, 0, 0, axis_index_groups=Z_GROUPS)
    both = jnp.stack([dy_copies[0], dy_next])
    grads = [both] + [to_x(both, d) for d in range(1, 4)]
    weights = [packed[0], near[0], far, near[1]]
    *grads, terms = lax.optimization_barrier((*grads, terms))
    (terms,) = call(sum_z_kernel, [((8, 16, 1792), BF)], z_odd, terms, scalars=1)
    mine, theirs = call(
        input_grad_kernel,
        [((2, 4, 64, 256), F32), ((2, 4, 64, 256), F32)],
        core,
        *weights,
        *grads,
        scalars=1,
        scratch=[pltpu.VMEM((128, 256), F32)],
    )
    terms = lax.all_to_all(terms, DS, 0, 0, axis_index_groups=Z_GROUPS)
    theirs = to_partner(theirs)
    mine, theirs, terms = lax.optimization_barrier((mine, theirs, terms))
    terms = lax.all_to_all(jnp.broadcast_to(terms[None], (4, 8, 16, 1792)), DS, 0, 0, axis_index_groups=Y_GROUPS)
    grad_w, grad_b = call(filter_out_kernel, [((64, 13824), F32), ((64, 1), F32)], terms)
    (grad_x,) = call(join_kernel, [((2, 64, 1024), BF)], mine, theirs, matrix)
    return (
        activation.reshape(1, 1, 64, 256),
        grad_x.reshape(1, 2, 64, 1024),
        grad_w,
        grad_b.reshape(64),
    )


def solution(mesh):
    in_specs = (
        P("dp", "space", "chan", None),
        P("chan", None),
        P("chan"),
        P("dp", "space", "chan", None),
    )
    out_specs = (
        P("dp", "space", "chan", None),
        P("dp", "space", "chan", None),
        P("chan", None),
        P("chan"),
    )
    return jax.shard_map(
        per_device, mesh=mesh, in_specs=in_specs, out_specs=out_specs, check_vma=False
    )
```

```python
import jax
import jax.numpy as jnp
import numpy as np
from jax import lax
from jax.experimental import pallas as pl
from jax.experimental.pallas import tpu as pltpu
from jax.sharding import PartitionSpec as P

BF = jnp.bfloat16
F32 = jnp.float32
DS = ("dp", "space")
ALL = ("dp", "space", "chan")
Y_GROUPS = [[dp * 16 + z * 2 + yh for yh in range(2) for dp in range(2)] for z in range(8)]
Z_GROUPS = [[dp * 16 + z * 2 + yh for z in range(8)] for yh in range(2) for dp in range(2)]
YC_GROUPS = [
    [((dp * 16 + z * 2 + yh) * 8 + 2 * x + core) for yh in range(2) for dp in range(2) for core in range(2)]
    for z in range(8)
    for x in range(4)
]
ZC_GROUPS = [
    [((dp * 16 + z * 2 + yh) * 8 + 2 * x + core) for z in range(8) for core in range(2)]
    for yh in range(2)
    for dp in range(2)
    for x in range(4)
]
X_GROUPS = [[2 * x + core for x in range(4)] for core in range(2)]
TAP_OF = {(0, 0): 1, (1, 0): 2, (1, 1): 0}
PARAMS = pltpu.CompilerParams(vmem_limit_bytes=48 * 1024 * 1024)


def split_matrix():
    matrix = np.zeros((512, 512), np.float32)
    for y in range(16):
        for z in range(32):
            matrix[y * 32 + z, (2 * (y % 2) + z % 2) * 128 + (y // 2) * 16 + z // 2] = 1
    return matrix


def class_shifts(c):
    py, pz = c // 2, c % 2
    return [(sy, sz) for sy in range(py + 1) for sz in range(pz + 1)]


def taps_of(c):
    py, pz = c // 2, c % 2
    return [(TAP_OF[py, sy] * 3 + TAP_OF[pz, sz], sy, sz) for sy, sz in class_shifts(c)]


def lanes(shape):
    return lax.broadcasted_iota(jnp.int32, shape, 1)


def later(a, sy, sz):
    lane = lanes(a.shape)
    if sy:
        a = jnp.where(lane < 16, 0.0, pltpu.roll(a, 16, 1))
    if sz:
        a = jnp.where(lane % 16 == 0, 0.0, pltpu.roll(a, 1, 1))
    return a


def earlier(a, sy, sz):
    lane = lanes(a.shape)
    width = a.shape[1]
    if sy:
        a = jnp.where(lane % 256 >= 240, 0.0, pltpu.roll(a, width - 16, 1))
    if sz:
        a = jnp.where(lane % 16 == 15, 0.0, pltpu.roll(a, width - 1, 1))
    return a


def split_kernel(x_ref, m_ref, o_ref):
    for p in range(2):
        for h in range(2):
            r = jnp.dot(x_ref[p, :, h * 512 : (h + 1) * 512], m_ref[...], preferred_element_type=F32).astype(BF)
            for c in range(4):
                for copy in range(4):
                    o_ref[copy, p, c, :, h * 128 : (h + 1) * 128] = r[:, c * 128 : (c + 1) * 128]


def halves(a, b):
    low = lanes(a.shape) < 64
    return jnp.where(low, a, pltpu.roll(b, 64, 1)), jnp.where(low, pltpu.roll(a, 64, 1), b)


def core_pack_kernel(core_ref, w_ref, keep_ref, send_ref):
    first = core_ref[0] == 0
    for tap in range(27):
        for pair in range(2):
            at = tap * 512 + pair * 256
            low, high = halves(w_ref[:, at : at + 128].astype(F32), w_ref[:, at + 128 : at + 256].astype(F32))
            to = tap * 256 + pair * 128
            keep_ref[:, to : to + 128] = jnp.where(first, low, high).astype(BF)
            send_ref[:, to : to + 128] = jnp.where(first, high, low).astype(BF)


def forward_kernel(x_ref, w_ref, v_ref, mine_ref, theirs_ref, next_ref, next_theirs_ref):
    own = {}
    following = {}

    def add(table, key, value):
        table[key] = table[key] + value if key in table else value

    for c in range(4):
        taps = taps_of(c)
        for p, firsts in ((1, (0, 2)), (0, (1,))):
            rows = []
            for k1 in firsts:
                for tap, _, _ in taps:
                    at = (9 * k1 + tap) * 256
                    rows += [w_ref[:, at : at + 256], v_ref[:, at : at + 256]]
            cells = jnp.concatenate([x_ref[x, p, c] for x in range(4)], 0)
            r = jnp.dot(jnp.concatenate(rows, 0), cells, preferred_element_type=F32)
            n = 0
            for k1 in firsts:
                for _, sy, sz in taps:
                    add(following if k1 == 0 else own, (sy, sz), r[128 * n : 128 * n + 128])
                    n += 1
    total = sum(later(v, *s) for s, v in own.items())
    mine_ref[...] = total[:64]
    theirs_ref[...] = total[64:]
    total = sum(later(v, *s) for s, v in following.items())
    next_ref[...] = total[:64]
    next_theirs_ref[...] = total[64:]


def gelu_kernel(a_ref, b_ref, c_ref, d_ref, bias_ref, g_ref, act_ref, dy_ref):
    u = ((a_ref[...] + b_ref[...]) + (c_ref[...] + d_ref[...])) + bias_ref[...]
    root = float(np.sqrt(2 / np.pi))
    t = jnp.tanh(root * (u + 0.044715 * (u * u * u)))
    act_ref[...] = (0.5 * u * (1.0 + t)).astype(BF)
    slope = 0.5 * (1.0 + t) + 0.5 * u * (1.0 - t * t) * (root * (1.0 + 3 * 0.044715 * (u * u)))
    dy = (g_ref[...].astype(F32) * slope).astype(BF)
    for copy in range(8):
        dy_ref[copy] = dy


def with_pair(block, total):
    hi = total.astype(BF).astype(F32)
    lane = lanes(block.shape)
    pair = jnp.where(lane == 64, hi, jnp.where(lane == 65, total - hi, 0.0))
    return jnp.where(lane < 64, block, pair).astype(BF)


def filter_grad_kernel(dy_ref, x_ref, e_ref, o_ref, xs_ref):
    for c in range(4):
        for y in range(4):
            cells = slice(y * 256, y * 256 + 256)
            xs_ref[c, 0:64, cells] = x_ref[y, 0, c]
            xs_ref[c, 64:128, cells] = x_ref[y, 1, c]
            xs_ref[c, 128:192, cells] = e_ref[y, c] if y < 2 else x_ref[y - 2, 1, c]
    grads = jnp.concatenate(
        [jnp.concatenate([dy_ref[2 * y + core] for y in range(4)], 1) for core in range(2)], 0
    ).astype(F32)
    shifted = {(sy, sz): earlier(grads, sy, sz).astype(BF) for sy in range(2) for sz in range(2)}

    def put(n, block):
        h, at = divmod(n, 7)
        for core in range(2):
            for fb in range(4):
                row = core * 64 + fb * 16
                o_ref[4 * fb + 2 * h + core, :, at * 128 : at * 128 + 128] = block[row : row + 16]

    firsts = {}
    for c in range(4):
        taps = taps_of(c)
        r = lax.dot_general(
            jnp.concatenate([shifted[sy, sz] for _, sy, sz in taps], 0),
            xs_ref[c],
            (((1,), (1,)), ((), ())),
            preferred_element_type=F32,
        )
        for n, (tap, _, _) in enumerate(taps):
            put(tap, r[128 * n : 128 * n + 128, 0:128].astype(BF))
            firsts[tap] = r[128 * n : 128 * n + 128, 128:192]
    for j in range(4):
        put(9 + j, jnp.concatenate([firsts[2 * j], firsts[2 * j + 1]], 1).astype(BF))
    last = jnp.concatenate([firsts[8], jnp.zeros((128, 64), F32)], 1)
    put(13, with_pair(last, jnp.sum(grads, 1, keepdims=True)))


def sum_z_kernel(odd_ref, r_ref, o_ref):
    for core in range(2):
        for at in range(0, 896, 128):
            total = sum(r_ref[2 * s + core, :, at : at + 128].astype(F32) for s in range(8))
            out = total.astype(BF)
            if at == 768:
                both = total[:, 64:65] + total[:, 65:66]
                out = jnp.where(odd_ref[0] == 1, with_pair(total, both).astype(F32), out.astype(F32)).astype(BF)
            for copy in range(8):
                o_ref[copy, core, :, at : at + 128] = out


def filter_out_kernel(q_ref, own_ref, back_ref, ahead_ref, c_ref, d_ref, w_ref, b_ref):
    q = q_ref[0]
    for source, refs in ((0, (own_ref,)), (3, (back_ref,)), (1, (ahead_ref,)), (2, (c_ref, d_ref))):
        to = lax.rem(q + source, 4) * 128
        for fb in range(4):
            rows = slice(fb * 16, fb * 16 + 16)
            for n in range(14):
                h, at = divmod(n, 7)
                z = 2 * fb + h
                ref = refs[0] if len(refs) == 1 or z < 4 else refs[1]
                z = z if len(refs) == 1 else z % 4
                a = ref[z, 0, :, at * 128 : at * 128 + 128].astype(F32) * 0.5
                b = ref[z, 1, :, at * 128 : at * 128 + 128].astype(F32) * 0.5
                low, high = halves(a, b)
                taps = (9 + n, 18 + n) if n < 9 else (2 * n - 18, 2 * n - 17)
                w_ref[rows, pl.ds(pl.multiple_of(taps[0] * 512 + to, 128), 128)] = low
                if n < 13:
                    w_ref[rows, pl.ds(pl.multiple_of(taps[1] * 512 + to, 128), 128)] = high
                elif source == 0:
                    b_ref[rows, :] = a[:, 64:65] + a[:, 65:66]


def pack_kernel(x_ref, w_ref, *o_refs):
    for d in range(4):
        to = lax.rem(x_ref[0] + d, 4) * 128
        for tap in range(27):
            o_refs[d][:, tap * 128 : tap * 128 + 128] = w_ref[:, pl.ds(pl.multiple_of(tap * 512 + to, 128), 128)]


def input_grad_kernel(core_ref, *refs):
    w_refs, d_refs, (mine_ref, theirs_ref), (g_ref,) = refs[:4], refs[4:8], refs[8:10], refs[10:]
    shifted = {}
    for which in range(2):
        full = jnp.concatenate([d[which] for d in d_refs], 0).astype(F32)
        for sy in range(2):
            for sz in range(2):
                shifted[which, sy, sz] = earlier(full, sy, sz).astype(BF)
    mine = pl.multiple_of(core_ref[0] * 64, 64)
    other = pl.multiple_of(64 - core_ref[0] * 64, 64)
    for c in range(4):
        for p, firsts in ((0, (1,)), (1, (2, 0))):
            total = None
            for k1 in firsts:
                for tap, sy, sz in taps_of(c):
                    at = (9 * k1 + tap) * 128
                    w = jnp.concatenate([w[:, at : at + 128] for w in w_refs], 0)
                    r = lax.dot_general(
                        w, shifted[1 if k1 == 0 else 0, sy, sz], (((0,), (0,)), ((), ())), preferred_element_type=F32
                    )
                    total = r if total is None else total + r
            g_ref[...] = total
            mine_ref[p, c] = g_ref[pl.ds(mine, 64), :]
            theirs_ref[p, c] = g_ref[pl.ds(other, 64), :]


def join_kernel(a_ref, b_ref, m_ref, o_ref):
    for p in range(2):
        for h in range(2):
            at = slice(h * 128, h * 128 + 128)
            parts = [(a_ref[p, c, :, at] + b_ref[p, c, :, at]).astype(BF) for c in range(4)]
            r = lax.dot_general(
                jnp.concatenate(parts, 1), m_ref[...], (((1,), (1,)), ((), ())), preferred_element_type=F32
            )
            o_ref[p, :, h * 512 : (h + 1) * 512] = r.astype(BF)


VMEM = pl.BlockSpec(memory_space=pltpu.VMEM)
SMEM = pl.BlockSpec(memory_space=pltpu.SMEM)


def call(kernel, outs, *args, scalars=0, scratch=()):
    shapes = [jax.ShapeDtypeStruct(s, t) for s, t in outs]
    result = pl.pallas_call(
        kernel,
        out_shape=shapes,
        in_specs=[SMEM] * scalars + [VMEM] * (len(args) - scalars),
        out_specs=[VMEM] * len(outs),
        scratch_shapes=list(scratch),
        compiler_params=PARAMS,
    )(*args)
    return result


def shift_space(a, by):
    return lax.ppermute(a, "space", [(i, i + by) for i in range(16) if 0 <= i + by < 16])


def to_x(a, d):
    return lax.ppermute(a, "chan", [(i, (i + 2 * d) % 8) for i in range(8)])


def over_y(a, by):
    pairs = []
    for i in range(32):
        dp, z, yh = i // 16, i % 16 // 2, i % 2
        y = (2 * yh + dp + by) % 4
        pairs.append((i, y % 2 * 16 + 2 * z + y // 2))
    return lax.ppermute(a, DS, pairs)


def next_partner(a):
    pairs = []
    for i in range(256):
        chan, space, dp = i % 8, i // 8 % 16, i // 128
        if space < 15:
            pairs.append((i, (dp * 16 + space + 1) * 8 + (chan ^ 1)))
    return lax.ppermute(a, ALL, pairs)


def to_partner(a):
    return lax.ppermute(a, "chan", [(i, i ^ 1) for i in range(8)])


def per_device(volumes, kernel, bias, act_grad):
    chan = lax.axis_index("chan")
    core = (chan % 2).astype(jnp.int32).reshape(1)
    x = (chan // 2).astype(jnp.int32).reshape(1)
    z_odd = ((lax.axis_index("space") // 2) % 2).astype(jnp.int32).reshape(1)
    matrix = jnp.asarray(split_matrix(), BF)

    q = ((lax.axis_index("space") % 2) * 2 + lax.axis_index("dp")).astype(jnp.int32).reshape(1)

    (copies,) = call(split_kernel, [((4, 2, 4, 64, 256), BF)], volumes.reshape(2, 64, 1024), matrix)
    w_keep, w_send = call(core_pack_kernel, [((64, 6912), BF)] * 2, core, kernel, scalars=1)
    w_other = to_partner(w_send)
    x_own = lax.all_to_all(copies, "chan", 0, 0, axis_index_groups=X_GROUPS)
    packed = call(pack_kernel, [((64, 3456), BF)] * 4, x, kernel, scalars=1)
    *packed, x_own = lax.optimization_barrier((*packed, x_own))
    ring = lax.all_to_all(x_own, DS, 0, 0, axis_index_groups=Y_GROUPS)
    far = [to_x(packed[d], d) for d in range(1, 4)]
    mine, theirs, following, following_theirs = call(
        forward_kernel, [((64, 256), F32)] * 4, x_own, w_keep, w_other
    )
    parts = (mine, to_partner(theirs), shift_space(following, 1), next_partner(following_theirs))
    activation, dy_copies = call(
        gelu_kernel,
        [((64, 256), BF), ((8, 64, 256), BF)],
        *parts,
        bias.reshape(64, 1),
        act_grad.reshape(64, 256),
    )
    ring, _ = lax.optimization_barrier((ring, parts[2]))
    edge = shift_space(ring[2:, 1], 2)
    dy = lax.all_to_all(dy_copies, ALL, 0, 0, axis_index_groups=YC_GROUPS)
    dy_next = shift_space(dy_copies[0], -1)
    (terms,) = call(
        filter_grad_kernel, [((16, 16, 896), BF)], dy, ring, edge, scratch=[pltpu.VMEM((4, 192, 1024), BF)]
    )
    *far, terms, dy_next = lax.optimization_barrier((*far, terms, dy_next))
    terms = lax.all_to_all(terms, ALL, 0, 0, axis_index_groups=ZC_GROUPS)
    both = jnp.stack([dy_copies[0], dy_next])
    grads = [both] + [to_x(both, d) for d in range(1, 4)]
    *grads, terms = lax.optimization_barrier((*grads, terms))
    (terms,) = call(sum_z_kernel, [((8, 2, 16, 896), BF)], z_odd, terms, scalars=1)
    mine, theirs = call(
        input_grad_kernel,
        [((2, 4, 64, 256), F32), ((2, 4, 64, 256), F32)],
        core,
        packed[0],
        *far,
        *grads,
        scalars=1,
        scratch=[pltpu.VMEM((128, 256), F32)],
    )
    terms = lax.all_to_all(terms, DS, 0, 0, axis_index_groups=Z_GROUPS)
    theirs = to_partner(theirs)
    mine, theirs, terms = lax.optimization_barrier((mine, theirs, terms))
    back, ahead = over_y(terms, 1), over_y(terms, -1)
    (grad_x,) = call(join_kernel, [((2, 64, 1024), BF)], mine, theirs, matrix)
    grad_w, grad_b = call(
        filter_out_kernel,
        [((64, 13824), F32), ((64, 1), F32)],
        q,
        terms,
        back,
        ahead,
        over_y(back[:4], 1),
        over_y(ahead[4:], -1),
        scalars=1,
    )
    return (
        activation.reshape(1, 1, 64, 256),
        grad_x.reshape(1, 2, 64, 1024),
        grad_w,
        grad_b.reshape(64),
    )


def solution(mesh):
    in_specs = (
        P("dp", "space", "chan", None),
        P("chan", None),
        P("chan"),
        P("dp", "space", "chan", None),
    )
    out_specs = (
        P("dp", "space", "chan", None),
        P("dp", "space", "chan", None),
        P("chan", None),
        P("chan"),
    )
    return jax.shard_map(
        per_device, mesh=mesh, in_specs=in_specs, out_specs=out_specs, check_vma=False
    )
```

```python
import functools

import jax
import jax.numpy as jnp
import numpy as np
from jax import lax
from jax.experimental import pallas as pl
from jax.experimental.pallas import tpu as pltpu
from jax.sharding import PartitionSpec as P

BF = jnp.bfloat16
F32 = jnp.float32
DS = ("dp", "space")
ALL = ("dp", "space", "chan")
Y_GROUPS = [[dp * 16 + z * 2 + yh for yh in range(2) for dp in range(2)] for z in range(8)]
Z_GROUPS = [[dp * 16 + z * 2 + yh for z in range(8)] for yh in range(2) for dp in range(2)]
YC_GROUPS = [
    [((dp * 16 + z * 2 + yh) * 8 + 2 * x + core) for yh in range(2) for dp in range(2) for core in range(2)]
    for z in range(8)
    for x in range(4)
]
ZC_GROUPS = [
    [((dp * 16 + z * 2 + yh) * 8 + 2 * x + core) for z in range(8) for core in range(2)]
    for yh in range(2)
    for dp in range(2)
    for x in range(4)
]
X_GROUPS = [[2 * x + core for x in range(4)] for core in range(2)]
TAP_OF = {(0, 0): 1, (1, 0): 2, (1, 1): 0}
PARAMS = pltpu.CompilerParams(vmem_limit_bytes=48 * 1024 * 1024)


def split_matrix():
    matrix = np.zeros((512, 512), np.float32)
    for y in range(16):
        for z in range(32):
            matrix[y * 32 + z, (2 * (y % 2) + z % 2) * 128 + (y // 2) * 16 + z // 2] = 1
    return matrix


def class_shifts(c):
    py, pz = c // 2, c % 2
    return [(sy, sz) for sy in range(py + 1) for sz in range(pz + 1)]


def taps_of(c):
    py, pz = c // 2, c % 2
    return [(TAP_OF[py, sy] * 3 + TAP_OF[pz, sz], sy, sz) for sy, sz in class_shifts(c)]


def lanes(shape):
    return lax.broadcasted_iota(jnp.int32, shape, 1)


def later(a, sy, sz):
    lane = lanes(a.shape)
    if sy:
        a = jnp.where(lane < 16, 0.0, pltpu.roll(a, 16, 1))
    if sz:
        a = jnp.where(lane % 16 == 0, 0.0, pltpu.roll(a, 1, 1))
    return a


def earlier(a, sy, sz):
    lane = lanes(a.shape)
    width = a.shape[1]
    if sy:
        a = jnp.where(lane % 256 >= 240, 0.0, pltpu.roll(a, width - 16, 1))
    if sz:
        a = jnp.where(lane % 16 == 15, 0.0, pltpu.roll(a, width - 1, 1))
    return a


def split_kernel(x_ref, m_ref, o_ref):
    for p in range(2):
        for h in range(2):
            r = jnp.dot(x_ref[p, :, h * 512 : (h + 1) * 512], m_ref[...], preferred_element_type=F32).astype(BF)
            for c in range(4):
                for copy in range(4):
                    o_ref[copy, p, c, :, h * 128 : (h + 1) * 128] = r[:, c * 128 : (c + 1) * 128]


def halves(a, b):
    low = lanes(a.shape) < 64
    return jnp.where(low, a, pltpu.roll(b, 64, 1)), jnp.where(low, pltpu.roll(a, 64, 1), b)


def core_pack_kernel(core_ref, w_ref, keep_ref, send_ref):
    first = core_ref[0] == 0
    for tap in range(27):
        for pair in range(2):
            at = tap * 512 + pair * 256
            low, high = halves(w_ref[:, at : at + 128].astype(F32), w_ref[:, at + 128 : at + 256].astype(F32))
            to = tap * 256 + pair * 128
            keep_ref[:, to : to + 128] = jnp.where(first, low, high).astype(BF)
            send_ref[:, to : to + 128] = jnp.where(first, high, low).astype(BF)


def forward_kernel(choice, x_ref, w_ref, v_ref, mine_ref, theirs_ref):
    sums = {}
    for c in range(4):
        taps = taps_of(c)
        for p, k1 in choice:
            rows = []
            for tap, _, _ in taps:
                at = (9 * k1 + tap) * 256
                rows += [w_ref[:, at : at + 256], v_ref[:, at : at + 256]]
            cells = jnp.concatenate([x_ref[x, p, c] for x in range(4)], 0)
            r = jnp.dot(jnp.concatenate(rows, 0), cells, preferred_element_type=F32)
            for n, (_, sy, sz) in enumerate(taps):
                value = r[128 * n : 128 * n + 128]
                sums[sy, sz] = sums[sy, sz] + value if (sy, sz) in sums else value
    total = sum(later(v, *s) for s, v in sums.items())
    mine_ref[...] = total[:64]
    theirs_ref[...] = total[64:]


def gelu_kernel(a_ref, b_ref, c_ref, bias_ref, g_ref, act_ref, one_ref, dy_ref):
    u = ((a_ref[...] + b_ref[...]) + c_ref[...]) + bias_ref[...]
    root = float(np.sqrt(2 / np.pi))
    t = jnp.tanh(root * (u + 0.044715 * (u * u * u)))
    act_ref[...] = (0.5 * u * (1.0 + t)).astype(BF)
    slope = 0.5 * (1.0 + t) + 0.5 * u * (1.0 - t * t) * (root * (1.0 + 3 * 0.044715 * (u * u)))
    dy = (g_ref[...].astype(F32) * slope).astype(BF)
    one_ref[...] = dy
    for copy in range(8):
        dy_ref[copy] = dy


def with_pair(block, total):
    hi = total.astype(BF).astype(F32)
    lane = lanes(block.shape)
    pair = jnp.where(lane == 64, hi, jnp.where(lane == 65, total - hi, 0.0))
    return jnp.where(lane < 64, block, pair).astype(BF)


def filter_grad_kernel(dy_ref, x_ref, e_ref, o_ref, xs_ref):
    for c in range(4):
        for y in range(4):
            cells = slice(y * 256, y * 256 + 256)
            xs_ref[c, 0:64, cells] = x_ref[y, 0, c]
            xs_ref[c, 64:128, cells] = x_ref[y, 1, c]
            xs_ref[c, 128:192, cells] = e_ref[y, c] if y < 2 else x_ref[y - 2, 1, c]
    grads = jnp.concatenate(
        [jnp.concatenate([dy_ref[2 * y + core] for y in range(4)], 1) for core in range(2)], 0
    ).astype(F32)
    shifted = {(sy, sz): earlier(grads, sy, sz).astype(BF) for sy in range(2) for sz in range(2)}

    def put(n, block):
        h, at = divmod(n, 7)
        for core in range(2):
            for fb in range(4):
                row = core * 64 + fb * 16
                o_ref[4 * fb + 2 * h + core, :, at * 128 : at * 128 + 128] = block[row : row + 16]

    firsts = {}
    for c in range(4):
        taps = taps_of(c)
        r = lax.dot_general(
            jnp.concatenate([shifted[sy, sz] for _, sy, sz in taps], 0),
            xs_ref[c],
            (((1,), (1,)), ((), ())),
            preferred_element_type=F32,
        )
        for n, (tap, _, _) in enumerate(taps):
            put(tap, r[128 * n : 128 * n + 128, 0:128].astype(BF))
            firsts[tap] = r[128 * n : 128 * n + 128, 128:192]
    for j in range(4):
        put(9 + j, jnp.concatenate([firsts[2 * j], firsts[2 * j + 1]], 1).astype(BF))
    last = jnp.concatenate([firsts[8], jnp.zeros((128, 64), F32)], 1)
    put(13, with_pair(last, jnp.sum(grads, 1, keepdims=True)))


def sum_z_kernel(odd_ref, r_ref, o_ref):
    for core in range(2):
        for at in range(0, 896, 128):
            total = sum(r_ref[2 * s + core, :, at : at + 128].astype(F32) for s in range(8))
            out = total.astype(BF)
            if at == 768:
                both = total[:, 64:65] + total[:, 65:66]
                out = jnp.where(odd_ref[0] == 1, with_pair(total, both).astype(F32), out.astype(F32)).astype(BF)
            for copy in range(8):
                o_ref[copy, core, :, at : at + 128] = out


def cut_kernel(r_ref, a_ref, b_ref):
    a_ref[...] = r_ref[:4]
    b_ref[...] = r_ref[4:]


def place(first, second, store, bias):
    for z in range(8):
        fb, h = divmod(z, 2)
        ref = first if z < 4 else second
        rows = slice(fb * 16, fb * 16 + 16)
        for at in range(7):
            n = 7 * h + at
            a = ref[z % 4, 0, :, at * 128 : at * 128 + 128].astype(F32) * 0.5
            b = ref[z % 4, 1, :, at * 128 : at * 128 + 128].astype(F32) * 0.5
            low, high = halves(a, b)
            taps = (9 + n, 18 + n) if n < 9 else (2 * n - 18, 2 * n - 17)
            store(rows, taps[0], low)
            if n < 13:
                store(rows, taps[1], high)
            elif bias is not None:
                bias[rows, :] = a[:, 64:65] + a[:, 65:66]


def filter_out_kernel(q_ref, o0, o1, a0, a1, b0, b1, w_ref, b_ref):
    def at(tap, source):
        to = lax.rem(q_ref[0] + source, 4) * 128
        return pl.ds(pl.multiple_of(tap * 512 + to, 128), 128)

    for source, first, second in ((0, o0, o1), (3, a0, a1), (1, b0, b1)):

        def store(rows, tap, value, source=source):
            w_ref[rows, at(tap, source)] = value

        place(first, second, store, b_ref if source == 0 else None)
    for tap in range(27):
        w_ref[:, at(tap, 2)] = jnp.zeros((64, 128), F32)


def filter_last_kernel(q_ref, c_ref, d_ref, w_in, w_ref, s_ref, sems):
    def store(rows, tap, value):
        s_ref[rows, tap * 128 : tap * 128 + 128] = value

    place(c_ref, d_ref, store, None)
    to = lax.rem(q_ref[0] + 2, 4) * 128
    copies = []
    for tap in range(27):
        copies.append(
            pltpu.make_async_copy(
                s_ref.at[:, pl.ds(tap * 128, 128)],
                w_ref.at[:, pl.ds(pl.multiple_of(tap * 512 + to, 128), 128)],
                sems.at[tap],
            )
        )
        copies[-1].start()
    for copy in copies:
        copy.wait()


def pack_kernel(x_ref, w_ref, *o_refs):
    for d in range(4):
        to = lax.rem(x_ref[0] + d, 4) * 128
        for tap in range(27):
            o_refs[d][:, tap * 128 : tap * 128 + 128] = w_ref[:, pl.ds(pl.multiple_of(tap * 512 + to, 128), 128)]


def input_grad_kernel(core_ref, *refs):
    w_refs, d_refs, (mine_ref, theirs_ref), (g_ref,) = refs[:4], refs[4:8], refs[8:10], refs[10:]
    shifted = {}
    for which in range(2):
        full = jnp.concatenate([d[which] for d in d_refs], 0).astype(F32)
        for sy in range(2):
            for sz in range(2):
                shifted[which, sy, sz] = earlier(full, sy, sz).astype(BF)
    mine = pl.multiple_of(core_ref[0] * 64, 64)
    other = pl.multiple_of(64 - core_ref[0] * 64, 64)
    for c in range(4):
        for p, firsts in ((0, (1,)), (1, (2, 0))):
            total = None
            for k1 in firsts:
                for tap, sy, sz in taps_of(c):
                    at = (9 * k1 + tap) * 128
                    w = jnp.concatenate([w[:, at : at + 128] for w in w_refs], 0)
                    r = lax.dot_general(
                        w, shifted[1 if k1 == 0 else 0, sy, sz], (((0,), (0,)), ((), ())), preferred_element_type=F32
                    )
                    total = r if total is None else total + r
            g_ref[...] = total
            mine_ref[p, c] = g_ref[pl.ds(mine, 64), :]
            theirs_ref[p, c] = g_ref[pl.ds(other, 64), :]


def join_kernel(a_ref, b_ref, m_ref, o_ref):
    for p in range(2):
        for h in range(2):
            at = slice(h * 128, h * 128 + 128)
            parts = [(a_ref[p, c, :, at] + b_ref[p, c, :, at]).astype(BF) for c in range(4)]
            r = lax.dot_general(
                jnp.concatenate(parts, 1), m_ref[...], (((1,), (1,)), ((), ())), preferred_element_type=F32
            )
            o_ref[p, :, h * 512 : (h + 1) * 512] = r.astype(BF)


VMEM = pl.BlockSpec(memory_space=pltpu.VMEM)
SMEM = pl.BlockSpec(memory_space=pltpu.SMEM)


def call(kernel, outs, *args, scalars=0, scratch=()):
    shapes = [jax.ShapeDtypeStruct(s, t) for s, t in outs]
    result = pl.pallas_call(
        kernel,
        out_shape=shapes,
        in_specs=[SMEM] * scalars + [VMEM] * (len(args) - scalars),
        out_specs=[VMEM] * len(outs),
        scratch_shapes=list(scratch),
        compiler_params=PARAMS,
    )(*args)
    return result


def shift_space(a, by):
    return lax.ppermute(a, "space", [(i, i + by) for i in range(16) if 0 <= i + by < 16])


def to_x(a, d):
    return lax.ppermute(a, "chan", [(i, (i + 2 * d) % 8) for i in range(8)])


def over_y(a, by):
    pairs = []
    for i in range(32):
        dp, z, yh = i // 16, i % 16 // 2, i % 2
        y = (2 * yh + dp + by) % 4
        pairs.append((i, y % 2 * 16 + 2 * z + y // 2))
    return lax.ppermute(a, DS, pairs)


def to_partner(a):
    return lax.ppermute(a, "chan", [(i, i ^ 1) for i in range(8)])


def per_device(volumes, kernel, bias, act_grad):
    chan = lax.axis_index("chan")
    core = (chan % 2).astype(jnp.int32).reshape(1)
    x = (chan // 2).astype(jnp.int32).reshape(1)
    z_odd = ((lax.axis_index("space") // 2) % 2).astype(jnp.int32).reshape(1)
    matrix = jnp.asarray(split_matrix(), BF)

    q = ((lax.axis_index("space") % 2) * 2 + lax.axis_index("dp")).astype(jnp.int32).reshape(1)

    (copies,) = call(split_kernel, [((4, 2, 4, 64, 256), BF)], volumes.reshape(2, 64, 1024), matrix)
    w_keep, w_send = call(core_pack_kernel, [((64, 6912), BF)] * 2, core, kernel, scalars=1)
    w_other = to_partner(w_send)
    x_own = lax.all_to_all(copies, "chan", 0, 0, axis_index_groups=X_GROUPS)
    packed = call(pack_kernel, [((64, 3456), BF)] * 4, x, kernel, scalars=1)
    *packed, x_own = lax.optimization_barrier((*packed, x_own))
    ring = lax.all_to_all(x_own, DS, 0, 0, axis_index_groups=Y_GROUPS)
    far = to_x(packed[2], 2)
    outs = [((64, 256), F32)] * 2
    following, theirs = call(functools.partial(forward_kernel, ((1, 0),)), outs, x_own, w_keep, w_other)
    following = shift_space(following + to_partner(theirs), 1)
    mine, theirs = call(functools.partial(forward_kernel, ((0, 1), (1, 2))), outs, x_own, w_keep, w_other)
    parts = (mine, to_partner(theirs), following)
    activation, dy_own, dy_copies = call(
        gelu_kernel,
        [((64, 256), BF), ((64, 256), BF), ((8, 64, 256), BF)],
        *parts,
        bias.reshape(64, 1),
        act_grad.reshape(64, 256),
    )
    ring, dy_own = lax.optimization_barrier((ring, dy_own))
    dy = lax.all_to_all(dy_copies, ALL, 0, 0, axis_index_groups=YC_GROUPS)
    edge = shift_space(ring[2:, 1], 2)
    dy_next = shift_space(dy_own, -1)
    (terms,) = call(
        filter_grad_kernel, [((16, 16, 896), BF)], dy, ring, edge, scratch=[pltpu.VMEM((4, 192, 1024), BF)]
    )
    far, dy_next, terms, *packed = lax.optimization_barrier((far, dy_next, terms, *packed))
    far = [to_x(packed[1], 1), far, to_x(packed[3], 3)]
    terms = lax.all_to_all(terms, ALL, 0, 0, axis_index_groups=ZC_GROUPS)
    both = jnp.stack([dy_own, dy_next])
    grads = [both] + [to_x(both, d) for d in range(1, 4)]
    *far, terms = lax.optimization_barrier((*far, terms))
    (terms,) = call(sum_z_kernel, [((8, 2, 16, 896), BF)], z_odd, terms, scalars=1)
    mine, theirs = call(
        input_grad_kernel,
        [((2, 4, 64, 256), F32), ((2, 4, 64, 256), F32)],
        core,
        packed[0],
        *far,
        *grads,
        scalars=1,
        scratch=[pltpu.VMEM((128, 256), F32)],
    )
    terms = lax.all_to_all(terms, DS, 0, 0, axis_index_groups=Z_GROUPS)
    theirs = to_partner(theirs)
    mine, theirs, terms = lax.optimization_barrier((mine, theirs, terms))
    half = call(cut_kernel, [((4, 2, 16, 896), BF)] * 2, terms)
    back = [over_y(half[0], 1), over_y(half[1], 1)]
    ahead = [over_y(half[0], -1), over_y(half[1], -1)]
    across = [over_y(back[0], 1), over_y(ahead[1], -1)]
    (grad_x,) = call(join_kernel, [((2, 64, 1024), BF)], mine, theirs, matrix)
    grad_w, grad_b = call(
        filter_out_kernel, [((64, 13824), F32), ((64, 1), F32)], q, *half, *back, *ahead, scalars=1
    )
    grad_w = pl.pallas_call(
        filter_last_kernel,
        out_shape=jax.ShapeDtypeStruct((64, 13824), F32),
        in_specs=[SMEM, VMEM, VMEM, pl.BlockSpec(memory_space=pl.ANY)],
        out_specs=pl.BlockSpec(memory_space=pl.ANY),
        scratch_shapes=[pltpu.VMEM((64, 3456), F32), pltpu.SemaphoreType.DMA((27,))],
        input_output_aliases={3: 0},
        compiler_params=PARAMS,
    )(q, *across, grad_w)
    return (
        activation.reshape(1, 1, 64, 256),
        grad_x.reshape(1, 2, 64, 1024),
        grad_w,
        grad_b.reshape(64),
    )


def solution(mesh):
    in_specs = (
        P("dp", "space", "chan", None),
        P("chan", None),
        P("chan"),
        P("dp", "space", "chan", None),
    )
    out_specs = (
        P("dp", "space", "chan", None),
        P("dp", "space", "chan", None),
        P("chan", None),
        P("chan"),
    )
    return jax.shard_map(
        per_device, mesh=mesh, in_specs=in_specs, out_specs=out_specs, check_vma=False
    )
```

```python
import functools

import jax
import jax.numpy as jnp
import numpy as np
from jax import lax
from jax.experimental import pallas as pl
from jax.experimental.pallas import tpu as pltpu
from jax.sharding import PartitionSpec as P

BF = jnp.bfloat16
F32 = jnp.float32
DS = ("dp", "space")
ALL = ("dp", "space", "chan")
Y_GROUPS = [[dp * 16 + z * 2 + yh for yh in range(2) for dp in range(2)] for z in range(8)]
Z_GROUPS = [[dp * 16 + z * 2 + yh for z in range(8)] for yh in range(2) for dp in range(2)]
YC_GROUPS = [
    [((dp * 16 + z * 2 + yh) * 8 + 2 * x + core) for yh in range(2) for dp in range(2) for core in range(2)]
    for z in range(8)
    for x in range(4)
]
ZC_GROUPS = [
    [((dp * 16 + z * 2 + yh) * 8 + 2 * x + core) for z in range(8) for core in range(2)]
    for yh in range(2)
    for dp in range(2)
    for x in range(4)
]
X_GROUPS = [[2 * x + core for x in range(4)] for core in range(2)]
TAP_OF = {(0, 0): 1, (1, 0): 2, (1, 1): 0}
PARAMS = pltpu.CompilerParams(vmem_limit_bytes=48 * 1024 * 1024)


def split_matrix():
    cell = lax.broadcasted_iota(jnp.int32, (512, 512), 0)
    lane = lax.broadcasted_iota(jnp.int32, (512, 512), 1)
    to = ((cell >> 5) & 1) * 256 + (cell & 1) * 128 + (cell >> 6) * 16 + ((cell & 31) >> 1)
    return jnp.where(lane == to, 1.0, 0.0).astype(BF)


def class_shifts(c):
    py, pz = c // 2, c % 2
    return [(sy, sz) for sy in range(py + 1) for sz in range(pz + 1)]


def taps_of(c):
    py, pz = c // 2, c % 2
    return [(TAP_OF[py, sy] * 3 + TAP_OF[pz, sz], sy, sz) for sy, sz in class_shifts(c)]


def lanes(shape):
    return lax.broadcasted_iota(jnp.int32, shape, 1)


def later(a, sy, sz):
    lane = lanes(a.shape)
    if sy:
        a = jnp.where(lane < 16, 0.0, pltpu.roll(a, 16, 1))
    if sz:
        a = jnp.where(lane % 16 == 0, 0.0, pltpu.roll(a, 1, 1))
    return a


def earlier(a, sy, sz):
    lane = lanes(a.shape)
    width = a.shape[1]
    if sy:
        a = jnp.where(lane % 256 >= 240, 0.0, pltpu.roll(a, width - 16, 1))
    if sz:
        a = jnp.where(lane % 16 == 15, 0.0, pltpu.roll(a, width - 1, 1))
    return a


def split_kernel(x_ref, o_ref):
    matrix = split_matrix()
    for p in range(2):
        for h in range(2):
            r = jnp.dot(x_ref[p, :, h * 512 : (h + 1) * 512], matrix, preferred_element_type=F32).astype(BF)
            for c in range(4):
                o_ref[p, c, :, h * 128 : (h + 1) * 128] = r[:, c * 128 : (c + 1) * 128]


def halves(a, b):
    low = lanes(a.shape) < 64
    return jnp.where(low, a, pltpu.roll(b, 64, 1)), jnp.where(low, pltpu.roll(a, 64, 1), b)


STEPS = (0, 3, 2, 1)


def core_pack_kernel(where_ref, w_ref, keep_ref, send_ref):
    first = where_ref[0] == 0
    starts = [lax.rem(where_ref[1] + step, 4) * 128 for step in STEPS]

    def block(tap, k):
        return w_ref[:, pl.ds(pl.multiple_of(tap * 512 + starts[k], 128), 128)].astype(F32)

    for tap in range(27):
        for pair in range(2):
            low, high = halves(block(tap, 2 * pair), block(tap, 2 * pair + 1))
            to = tap * 256 + pair * 128
            keep_ref[:, to : to + 128] = jnp.where(first, low, high).astype(BF)
            send_ref[:, to : to + 128] = jnp.where(first, high, low).astype(BF)


def in_order_kernel(x_ref, own_ref, back_ref, ahead_ref, across_0, across_1, o_ref):
    for step, ref in ((0, own_ref), (3, back_ref), (1, ahead_ref)):
        o_ref[lax.rem(x_ref[0] + step, 4)] = ref[...]
    for p, ref in enumerate((across_0, across_1)):
        o_ref[lax.rem(x_ref[0] + 2, 4), p] = ref[...]


def accumulate(sums, c, k1, w_ref, v_ref, cells):
    taps = taps_of(c)
    rows = []
    for tap, _, _ in taps:
        at = (9 * k1 + tap) * 256
        rows += [w_ref[:, at : at + 256], v_ref[:, at : at + 256]]
    r = jnp.dot(jnp.concatenate(rows, 0), jnp.concatenate(cells, 0), preferred_element_type=F32)
    for m, (_, sy, sz) in enumerate(taps):
        value = r[128 * m : 128 * m + 128]
        sums[sy, sz] = sums[sy, sz] + value if (sy, sz) in sums else value


def finish(sums, mine_ref, theirs_ref):
    total = sum(later(v, *s) for s, v in sums.items())
    mine_ref[...] = total[:64]
    theirs_ref[...] = total[64:]


def next_kernel(own_ref, back_ref, across_ref, ahead_ref, w_ref, v_ref, mine_ref, theirs_ref):
    sums = {}
    for c in range(4):
        accumulate(sums, c, 0, w_ref, v_ref, [own_ref[1, c], back_ref[1, c], across_ref[c], ahead_ref[1, c]])
    finish(sums, mine_ref, theirs_ref)


def forward_kernel(x_ref, all_ref, w_ref, v_ref, mine_ref, theirs_ref):
    sums = {}
    at = [lax.rem(x_ref[0] + step, 4) for step in STEPS]
    for c in range(4):
        for p in range(2):
            accumulate(sums, c, p + 1, w_ref, v_ref, [all_ref[i, p, c] for i in at])
    finish(sums, mine_ref, theirs_ref)


def gelu_kernel(a_ref, b_ref, c_ref, bias_ref, g_ref, act_ref, one_ref, dy_ref):
    u = ((a_ref[...] + b_ref[...]) + c_ref[...]) + bias_ref[...]
    root = float(np.sqrt(2 / np.pi))
    t = jnp.tanh(root * (u + 0.044715 * (u * u * u)))
    act_ref[...] = (0.5 * u * (1.0 + t)).astype(BF)
    slope = 0.5 * (1.0 + t) + 0.5 * u * (1.0 - t * t) * (root * (1.0 + 3 * 0.044715 * (u * u)))
    dy = (g_ref[...].astype(F32) * slope).astype(BF)
    one_ref[...] = dy
    for copy in range(8):
        dy_ref[copy] = dy


def with_pair(block, total):
    hi = total.astype(BF).astype(F32)
    lane = lanes(block.shape)
    pair = jnp.where(lane == 64, hi, jnp.where(lane == 65, total - hi, 0.0))
    return jnp.where(lane < 64, block, pair).astype(BF)


def filter_grad_kernel(dy_ref, x_ref, e_ref, o_ref, xs_ref):
    for c in range(4):
        for y in range(4):
            cells = slice(y * 256, y * 256 + 256)
            xs_ref[c, 0:64, cells] = x_ref[y, 0, c]
            xs_ref[c, 64:128, cells] = x_ref[y, 1, c]
            xs_ref[c, 128:192, cells] = e_ref[y, c] if y < 2 else x_ref[y - 2, 1, c]
    grads = jnp.concatenate(
        [jnp.concatenate([dy_ref[2 * y + core] for y in range(4)], 1) for core in range(2)], 0
    ).astype(F32)
    shifted = {(sy, sz): earlier(grads, sy, sz).astype(BF) for sy in range(2) for sz in range(2)}

    def put(n, block):
        h, at = divmod(n, 7)
        for core in range(2):
            for fb in range(4):
                row = core * 64 + fb * 16
                o_ref[4 * fb + 2 * h + core, :, at * 128 : at * 128 + 128] = block[row : row + 16]

    firsts = {}
    for c in range(4):
        taps = taps_of(c)
        r = lax.dot_general(
            jnp.concatenate([shifted[sy, sz] for _, sy, sz in taps], 0),
            xs_ref[c],
            (((1,), (1,)), ((), ())),
            preferred_element_type=F32,
        )
        for n, (tap, _, _) in enumerate(taps):
            put(tap, r[128 * n : 128 * n + 128, 0:128].astype(BF))
            firsts[tap] = r[128 * n : 128 * n + 128, 128:192]
    for j in range(4):
        put(9 + j, jnp.concatenate([firsts[2 * j], firsts[2 * j + 1]], 1).astype(BF))
    last = jnp.concatenate([firsts[8], jnp.zeros((128, 64), F32)], 1)
    put(13, with_pair(last, jnp.sum(grads, 1, keepdims=True)))


def sum_z_kernel(odd_ref, r_ref, o_ref):
    for core in range(2):
        for at in range(0, 896, 128):
            total = sum(r_ref[2 * s + core, :, at : at + 128].astype(F32) for s in range(8))
            out = total.astype(BF)
            if at == 768:
                both = total[:, 64:65] + total[:, 65:66]
                out = jnp.where(odd_ref[0] == 1, with_pair(total, both).astype(F32), out.astype(F32)).astype(BF)
            for copy in range(8):
                o_ref[copy, core, :, at : at + 128] = out


def cut_kernel(r_ref, a_ref, b_ref):
    a_ref[...] = r_ref[:4]
    b_ref[...] = r_ref[4:]


def place(first, second, store, bias):
    for z in range(8):
        fb, h = divmod(z, 2)
        ref = first if z < 4 else second
        rows = slice(fb * 16, fb * 16 + 16)
        for at in range(7):
            n = 7 * h + at
            a = ref[z % 4, 0, :, at * 128 : at * 128 + 128].astype(F32) * 0.5
            b = ref[z % 4, 1, :, at * 128 : at * 128 + 128].astype(F32) * 0.5
            low, high = halves(a, b)
            taps = (9 + n, 18 + n) if n < 9 else (2 * n - 18, 2 * n - 17)
            store(rows, taps[0], low)
            if n < 13:
                store(rows, taps[1], high)
            elif bias is not None:
                bias[rows, :] = a[:, 64:65] + a[:, 65:66]


def filter_out_kernel(sources, has_bias, q_ref, *refs):
    n = 2 * len(sources)
    ins = refs[:n]
    if has_bias:
        w_ref, b_ref, s_ref, sems = refs[n:]
    else:
        _, w_ref, s_ref, sems = refs[n:]
        b_ref = None
    copies = []
    for k, source in enumerate(sources):

        def store(rows, tap, value, k=k):
            s_ref[k, rows, tap * 128 : tap * 128 + 128] = value

        place(ins[2 * k], ins[2 * k + 1], store, b_ref)
        to = lax.rem(q_ref[0] + source, 4) * 128
        for tap in range(27):
            copies.append(
                pltpu.make_async_copy(
                    s_ref.at[k, :, pl.ds(tap * 128, 128)],
                    w_ref.at[:, pl.ds(pl.multiple_of(tap * 512 + to, 128), 128)],
                    sems.at[k * 27 + tap],
                )
            )
            copies[-1].start()
    for copy in copies:
        copy.wait()


def filter_out(sources, q, pieces, so_far=None):
    n = len(sources)
    anywhere = pl.BlockSpec(memory_space=pl.ANY)
    first = so_far is None
    shape = jax.ShapeDtypeStruct((64, 13824), F32)
    return pl.pallas_call(
        functools.partial(filter_out_kernel, sources, first),
        out_shape=[shape, jax.ShapeDtypeStruct((64, 1), F32)] if first else shape,
        in_specs=[SMEM] + [VMEM] * (2 * n) + ([] if first else [anywhere]),
        out_specs=[anywhere, VMEM] if first else anywhere,
        scratch_shapes=[pltpu.VMEM((n, 64, 3456), F32), pltpu.SemaphoreType.DMA((27 * n,))],
        input_output_aliases={} if first else {2 * n + 1: 0},
        compiler_params=PARAMS,
    )(q, *pieces, *([] if first else [so_far]))


def pack_kernel(x_ref, w_ref, *o_refs):
    for d in range(4):
        to = lax.rem(x_ref[0] + d, 4) * 128
        for tap in range(27):
            o_refs[d][:, tap * 128 : tap * 128 + 128] = w_ref[:, pl.ds(pl.multiple_of(tap * 512 + to, 128), 128)]


def input_grad_kernel(core_ref, *refs):
    w_refs, d_refs, (mine_ref, theirs_ref), (g_ref,) = refs[:4], refs[4:8], refs[8:10], refs[10:]
    shifted = {}
    for which in range(2):
        full = jnp.concatenate([d[which] for d in d_refs], 0).astype(F32)
        for sy in range(2):
            for sz in range(2):
                shifted[which, sy, sz] = earlier(full, sy, sz).astype(BF)
    mine = pl.multiple_of(core_ref[0] * 64, 64)
    other = pl.multiple_of(64 - core_ref[0] * 64, 64)
    for c in range(4):
        for p, firsts in ((0, (1,)), (1, (2, 0))):
            total = None
            for k1 in firsts:
                for tap, sy, sz in taps_of(c):
                    at = (9 * k1 + tap) * 128
                    w = jnp.concatenate([w[:, at : at + 128] for w in w_refs], 0)
                    r = lax.dot_general(
                        w, shifted[1 if k1 == 0 else 0, sy, sz], (((0,), (0,)), ((), ())), preferred_element_type=F32
                    )
                    total = r if total is None else total + r
            g_ref[...] = total
            mine_ref[p, c] = g_ref[pl.ds(mine, 64), :]
            theirs_ref[p, c] = g_ref[pl.ds(other, 64), :]


def join_kernel(a_ref, b_ref, o_ref):
    matrix = split_matrix()
    for p in range(2):
        for h in range(2):
            at = slice(h * 128, h * 128 + 128)
            parts = [(a_ref[p, c, :, at] + b_ref[p, c, :, at]).astype(BF) for c in range(4)]
            r = lax.dot_general(
                jnp.concatenate(parts, 1), matrix, (((1,), (1,)), ((), ())), preferred_element_type=F32
            )
            o_ref[p, :, h * 512 : (h + 1) * 512] = r.astype(BF)


VMEM = pl.BlockSpec(memory_space=pltpu.VMEM)
SMEM = pl.BlockSpec(memory_space=pltpu.SMEM)


def call(kernel, outs, *args, scalars=0, scratch=()):
    shapes = [jax.ShapeDtypeStruct(s, t) for s, t in outs]
    result = pl.pallas_call(
        kernel,
        out_shape=shapes,
        in_specs=[SMEM] * scalars + [VMEM] * (len(args) - scalars),
        out_specs=[VMEM] * len(outs),
        scratch_shapes=list(scratch),
        compiler_params=PARAMS,
    )(*args)
    return result


def shift_space(a, by):
    return lax.ppermute(a, "space", [(i, i + by) for i in range(16) if 0 <= i + by < 16])


def to_x(a, d):
    return lax.ppermute(a, "chan", [(i, (i + 2 * d) % 8) for i in range(8)])


def over_y(a, by):
    pairs = []
    for i in range(32):
        dp, z, yh = i // 16, i % 16 // 2, i % 2
        y = (2 * yh + dp + by) % 4
        pairs.append((i, y % 2 * 16 + 2 * z + y // 2))
    return lax.ppermute(a, DS, pairs)


def to_partner(a):
    return lax.ppermute(a, "chan", [(i, i ^ 1) for i in range(8)])


def per_device(volumes, kernel, bias, act_grad):
    chan = lax.axis_index("chan")
    core = (chan % 2).astype(jnp.int32).reshape(1)
    x = (chan // 2).astype(jnp.int32).reshape(1)
    z_odd = ((lax.axis_index("space") // 2) % 2).astype(jnp.int32).reshape(1)

    q = ((lax.axis_index("space") % 2) * 2 + lax.axis_index("dp")).astype(jnp.int32).reshape(1)

    (cells,) = call(split_kernel, [((2, 4, 64, 256), BF)], volumes.reshape(2, 64, 1024))
    w_keep, w_send = call(
        core_pack_kernel, [((64, 6912), BF)] * 2, jnp.concatenate([core, x]), kernel, scalars=1
    )
    back, ahead = to_x(cells, 1), to_x(cells, 3)
    across = to_x(ahead[0], 3), to_x(back[1], 1)
    w_other = to_partner(w_send)
    outs = [((64, 256), F32)] * 2
    following, theirs = call(next_kernel, outs, cells, back, across[1], ahead, w_keep, w_other)
    following = shift_space(following + to_partner(theirs), 1)
    (x_own,) = call(in_order_kernel, [((4, 2, 4, 64, 256), BF)], x, cells, back, ahead, *across, scalars=1)
    packed = call(pack_kernel, [((64, 3456), BF)] * 4, x, kernel, scalars=1)
    *packed, x_own = lax.optimization_barrier((*packed, x_own))
    ring = lax.all_to_all(x_own, DS, 0, 0, axis_index_groups=Y_GROUPS)
    far = to_x(packed[2], 2)
    mine, theirs = call(forward_kernel, outs, x, x_own, w_keep, w_other, scalars=1)
    parts = (mine, to_partner(theirs), following)
    activation, dy_own, dy_copies = call(
        gelu_kernel,
        [((64, 256), BF), ((64, 256), BF), ((8, 64, 256), BF)],
        *parts,
        bias.reshape(64, 1),
        act_grad.reshape(64, 256),
    )
    ring, dy_own = lax.optimization_barrier((ring, dy_own))
    dy = lax.all_to_all(dy_copies, ALL, 0, 0, axis_index_groups=YC_GROUPS)
    edge = shift_space(ring[2:, 1], 2)
    dy_next = shift_space(dy_own, -1)
    (terms,) = call(
        filter_grad_kernel, [((16, 16, 896), BF)], dy, ring, edge, scratch=[pltpu.VMEM((4, 192, 1024), BF)]
    )
    far, dy_next, terms, *packed = lax.optimization_barrier((far, dy_next, terms, *packed))
    far = [to_x(packed[1], 1), far, to_x(packed[3], 3)]
    terms = lax.all_to_all(terms, ALL, 0, 0, axis_index_groups=ZC_GROUPS)
    both = jnp.stack([dy_own, dy_next])
    grads = [both] + [to_x(both, d) for d in range(1, 4)]
    *far, terms = lax.optimization_barrier((*far, terms))
    (terms,) = call(sum_z_kernel, [((8, 2, 16, 896), BF)], z_odd, terms, scalars=1)
    mine, theirs = call(
        input_grad_kernel,
        [((2, 4, 64, 256), F32), ((2, 4, 64, 256), F32)],
        core,
        packed[0],
        *far,
        *grads,
        scalars=1,
        scratch=[pltpu.VMEM((128, 256), F32)],
    )
    terms = lax.all_to_all(terms, DS, 0, 0, axis_index_groups=Z_GROUPS)
    theirs = to_partner(theirs)
    mine, theirs, terms = lax.optimization_barrier((mine, theirs, terms))
    half = call(cut_kernel, [((4, 2, 16, 896), BF)] * 2, terms)
    back = [over_y(half[0], 1), over_y(half[1], 1)]
    ahead = [over_y(half[0], -1), over_y(half[1], -1)]
    across = [over_y(back[0], 1), over_y(ahead[1], -1)]
    (grad_x,) = call(join_kernel, [((2, 64, 1024), BF)], mine, theirs)
    grad_w, grad_b = filter_out((0,), q, half)
    grad_w = filter_out((3, 1), q, back + ahead, grad_w)
    grad_w = filter_out((2,), q, across, grad_w)
    return (
        activation.reshape(1, 1, 64, 256),
        grad_x.reshape(1, 2, 64, 1024),
        grad_w,
        grad_b.reshape(64),
    )


def solution(mesh):
    in_specs = (
        P("dp", "space", "chan", None),
        P("chan", None),
        P("chan"),
        P("dp", "space", "chan", None),
    )
    out_specs = (
        P("dp", "space", "chan", None),
        P("dp", "space", "chan", None),
        P("chan", None),
        P("chan"),
    )
    return jax.shard_map(
        per_device, mesh=mesh, in_specs=in_specs, out_specs=out_specs, check_vma=False
    )
```

```python
import functools

import jax
import jax.numpy as jnp
import numpy as np
from jax import lax
from jax.experimental import pallas as pl
from jax.experimental.pallas import tpu as pltpu
from jax.sharding import PartitionSpec as P

BF = jnp.bfloat16
F32 = jnp.float32
DS = ("dp", "space")
ALL = ("dp", "space", "chan")
Y_GROUPS = [[dp * 16 + z * 2 + yh for yh in range(2) for dp in range(2)] for z in range(8)]
Z_GROUPS = [[dp * 16 + z * 2 + yh for z in range(7, -1, -1)] for yh in range(2) for dp in range(2)]
YC_GROUPS = [
    [((dp * 16 + z * 2 + yh) * 8 + 2 * x + core) for yh in range(2) for dp in range(2) for core in range(2)]
    for z in range(8)
    for x in range(4)
]
ZC_GROUPS = [
    [((dp * 16 + z * 2 + yh) * 8 + 2 * x + core) for z in range(8) for core in range(2)]
    for yh in range(2)
    for dp in range(2)
    for x in range(4)
]
X_GROUPS = [[2 * x + core for x in range(4)] for core in range(2)]
TAP_OF = {(0, 0): 1, (1, 0): 2, (1, 1): 0}
PARAMS = pltpu.CompilerParams(vmem_limit_bytes=48 * 1024 * 1024)


def split_matrix():
    cell = lax.broadcasted_iota(jnp.int32, (512, 512), 0)
    lane = lax.broadcasted_iota(jnp.int32, (512, 512), 1)
    to = ((cell >> 5) & 1) * 256 + (cell & 1) * 128 + (cell >> 6) * 16 + ((cell & 31) >> 1)
    return jnp.where(lane == to, 1.0, 0.0).astype(BF)


def class_shifts(c):
    py, pz = c // 2, c % 2
    return [(sy, sz) for sy in range(py + 1) for sz in range(pz + 1)]


def taps_of(c):
    py, pz = c // 2, c % 2
    return [(TAP_OF[py, sy] * 3 + TAP_OF[pz, sz], sy, sz) for sy, sz in class_shifts(c)]


def lanes(shape):
    return lax.broadcasted_iota(jnp.int32, shape, 1)


def later(a, sy, sz):
    lane = lanes(a.shape)
    if sy:
        a = jnp.where(lane < 16, 0.0, pltpu.roll(a, 16, 1))
    if sz:
        a = jnp.where(lane % 16 == 0, 0.0, pltpu.roll(a, 1, 1))
    return a


def earlier(a, sy, sz):
    lane = lanes(a.shape)
    width = a.shape[1]
    if sy:
        a = jnp.where(lane % 256 >= 240, 0.0, pltpu.roll(a, width - 16, 1))
    if sz:
        a = jnp.where(lane % 16 == 15, 0.0, pltpu.roll(a, width - 1, 1))
    return a


def split_kernel(x_ref, o_ref):
    matrix = split_matrix()
    for p in range(2):
        for h in range(2):
            r = jnp.dot(x_ref[p, :, h * 512 : (h + 1) * 512], matrix, preferred_element_type=F32).astype(BF)
            for c in range(4):
                o_ref[p, c, :, h * 128 : (h + 1) * 128] = r[:, c * 128 : (c + 1) * 128]


def halves(a, b):
    low = lanes(a.shape) < 64
    return jnp.where(low, a, pltpu.roll(b, 64, 1)), jnp.where(low, pltpu.roll(a, 64, 1), b)


STEPS = (0, 3, 2, 1)


def core_pack_kernel(where_ref, w_ref, keep_ref, send_ref):
    first = where_ref[0] == 0
    starts = [lax.rem(where_ref[1] + step, 4) * 128 for step in STEPS]

    def block(tap, k):
        return w_ref[:, pl.ds(pl.multiple_of(tap * 512 + starts[k], 128), 128)].astype(F32)

    for tap in range(27):
        for pair in range(2):
            low, high = halves(block(tap, 2 * pair), block(tap, 2 * pair + 1))
            to = tap * 256 + pair * 128
            keep_ref[:, to : to + 128] = jnp.where(first, low, high).astype(BF)
            send_ref[:, to : to + 128] = jnp.where(first, high, low).astype(BF)


def in_order_kernel(x_ref, own_ref, back_ref, ahead_ref, across_0, across_1, o_ref):
    for step, ref in ((0, own_ref), (3, back_ref), (1, ahead_ref)):
        o_ref[lax.rem(x_ref[0] + step, 4)] = ref[...]
    for p, ref in enumerate((across_0, across_1)):
        o_ref[lax.rem(x_ref[0] + 2, 4), p] = ref[...]


def accumulate(sums, c, k1, w_ref, v_ref, cells):
    taps = taps_of(c)
    rows = []
    for tap, _, _ in taps:
        at = (9 * k1 + tap) * 256
        rows += [w_ref[:, at : at + 256], v_ref[:, at : at + 256]]
    r = jnp.dot(jnp.concatenate(rows, 0), jnp.concatenate(cells, 0), preferred_element_type=F32)
    for m, (_, sy, sz) in enumerate(taps):
        value = r[128 * m : 128 * m + 128]
        sums[sy, sz] = sums[sy, sz] + value if (sy, sz) in sums else value


def finish(sums, mine_ref, theirs_ref):
    total = sum(later(v, *s) for s, v in sums.items())
    mine_ref[...] = total[:64]
    theirs_ref[...] = total[64:]


def next_kernel(own_ref, back_ref, across_ref, ahead_ref, w_ref, v_ref, mine_ref, theirs_ref):
    sums = {}
    for c in range(4):
        accumulate(sums, c, 0, w_ref, v_ref, [own_ref[1, c], back_ref[1, c], across_ref[c], ahead_ref[1, c]])
    finish(sums, mine_ref, theirs_ref)


def forward_kernel(x_ref, all_ref, w_ref, v_ref, mine_ref, theirs_ref):
    sums = {}
    at = [lax.rem(x_ref[0] + step, 4) for step in STEPS]
    for c in range(4):
        for p in range(2):
            accumulate(sums, c, p + 1, w_ref, v_ref, [all_ref[i, p, c] for i in at])
    finish(sums, mine_ref, theirs_ref)


def gelu_kernel(a_ref, b_ref, c_ref, bias_ref, g_ref, act_ref, one_ref, dy_ref):
    u = ((a_ref[...] + b_ref[...]) + c_ref[...]) + bias_ref[...]
    root = float(np.sqrt(2 / np.pi))
    t = jnp.tanh(root * (u + 0.044715 * (u * u * u)))
    act_ref[...] = (0.5 * u * (1.0 + t)).astype(BF)
    slope = 0.5 * (1.0 + t) + 0.5 * u * (1.0 - t * t) * (root * (1.0 + 3 * 0.044715 * (u * u)))
    dy = (g_ref[...].astype(F32) * slope).astype(BF)
    one_ref[...] = dy
    for copy in range(8):
        dy_ref[copy] = dy


def with_pair(block, total):
    hi = total.astype(BF).astype(F32)
    lane = lanes(block.shape)
    pair = jnp.where(lane == 64, hi, jnp.where(lane == 65, total - hi, 0.0))
    return jnp.where(lane < 64, block, pair).astype(BF)


def filter_grad_kernel(dy_ref, x_ref, e_ref, o_ref, xs_ref):
    for c in range(4):
        for y in range(4):
            cells = slice(y * 256, y * 256 + 256)
            xs_ref[c, 0:64, cells] = x_ref[y, 0, c]
            xs_ref[c, 64:128, cells] = x_ref[y, 1, c]
            xs_ref[c, 128:192, cells] = e_ref[y, c] if y < 2 else x_ref[y - 2, 1, c]
    grads = jnp.concatenate(
        [jnp.concatenate([dy_ref[2 * y + core] for y in range(4)], 1) for core in range(2)], 0
    ).astype(F32)
    shifted = {(sy, sz): earlier(grads, sy, sz).astype(BF) for sy in range(2) for sz in range(2)}

    def put(n, block):
        h, at = divmod(n, 7)
        for core in range(2):
            for fb in range(4):
                row = core * 64 + fb * 16
                o_ref[4 * fb + 2 * h + core, :, at * 128 : at * 128 + 128] = block[row : row + 16]

    firsts = {}
    for c in range(4):
        taps = taps_of(c)
        r = lax.dot_general(
            jnp.concatenate([shifted[sy, sz] for _, sy, sz in taps], 0),
            xs_ref[c],
            (((1,), (1,)), ((), ())),
            preferred_element_type=F32,
        )
        for n, (tap, _, _) in enumerate(taps):
            put(tap, r[128 * n : 128 * n + 128, 0:128].astype(BF))
            firsts[tap] = r[128 * n : 128 * n + 128, 128:192]
    for j in range(4):
        put(9 + j, jnp.concatenate([firsts[2 * j], firsts[2 * j + 1]], 1).astype(BF))
    last = jnp.concatenate([firsts[8], jnp.zeros((128, 64), F32)], 1)
    put(13, with_pair(last, jnp.sum(grads, 1, keepdims=True)))


def sum_z_kernel(odd_ref, r_ref, o_ref):
    for core in range(2):
        for at in range(0, 896, 128):
            total = sum(r_ref[2 * s + core, :, at : at + 128].astype(F32) for s in range(8))
            out = total.astype(BF)
            if at == 768:
                both = total[:, 64:65] + total[:, 65:66]
                out = jnp.where(odd_ref[0] == 1, with_pair(total, both).astype(F32), out.astype(F32)).astype(BF)
            for copy in range(8):
                o_ref[copy, core, :, at : at + 128] = out


def cut_kernel(r_ref, a_ref, b_ref):
    for i in range(4):
        a_ref[i] = r_ref[7 - i]
        b_ref[i] = r_ref[3 - i]


def place(first, second, store, bias):
    for z in range(8):
        fb, h = divmod(z, 2)
        ref = first if z < 4 else second
        rows = slice(fb * 16, fb * 16 + 16)
        for at in range(7):
            n = 7 * h + at
            a = ref[z % 4, 0, :, at * 128 : at * 128 + 128].astype(F32) * 0.5
            b = ref[z % 4, 1, :, at * 128 : at * 128 + 128].astype(F32) * 0.5
            low, high = halves(a, b)
            taps = (9 + n, 18 + n) if n < 9 else (2 * n - 18, 2 * n - 17)
            store(rows, taps[0], low)
            if n < 13:
                store(rows, taps[1], high)
            elif bias is not None:
                bias[rows, :] = a[:, 64:65] + a[:, 65:66]


def filter_out_kernel(sources, has_bias, q_ref, *refs):
    n = 2 * len(sources)
    ins = refs[:n]
    if has_bias:
        w_ref, b_ref, s_ref, sems = refs[n:]
    else:
        _, w_ref, s_ref, sems = refs[n:]
        b_ref = None
    copies = []
    for k, source in enumerate(sources):

        def store(rows, tap, value, k=k):
            s_ref[k, rows, tap * 128 : tap * 128 + 128] = value

        place(ins[2 * k], ins[2 * k + 1], store, b_ref)
        to = lax.rem(q_ref[0] + source, 4) * 128
        for tap in range(27):
            copies.append(
                pltpu.make_async_copy(
                    s_ref.at[k, :, pl.ds(tap * 128, 128)],
                    w_ref.at[:, pl.ds(pl.multiple_of(tap * 512 + to, 128), 128)],
                    sems.at[k * 27 + tap],
                )
            )
            copies[-1].start()
    for copy in copies:
        copy.wait()


def filter_out(sources, q, pieces, so_far=None):
    n = len(sources)
    anywhere = pl.BlockSpec(memory_space=pl.ANY)
    first = so_far is None
    shape = jax.ShapeDtypeStruct((64, 13824), F32)
    return pl.pallas_call(
        functools.partial(filter_out_kernel, sources, first),
        out_shape=[shape, jax.ShapeDtypeStruct((64, 1), F32)] if first else shape,
        in_specs=[SMEM] + [VMEM] * (2 * n) + ([] if first else [anywhere]),
        out_specs=[anywhere, VMEM] if first else anywhere,
        scratch_shapes=[pltpu.VMEM((n, 64, 3456), F32), pltpu.SemaphoreType.DMA((27 * n,))],
        input_output_aliases={} if first else {2 * n + 1: 0},
        compiler_params=PARAMS,
    )(q, *pieces, *([] if first else [so_far]))


def pack_kernel(x_ref, w_ref, *o_refs):
    for d in range(4):
        to = lax.rem(x_ref[0] + d, 4) * 128
        for tap in range(27):
            o_refs[d][:, tap * 128 : tap * 128 + 128] = w_ref[:, pl.ds(pl.multiple_of(tap * 512 + to, 128), 128)]


def input_grad_kernel(core_ref, *refs):
    w_refs, d_refs, (mine_ref, theirs_ref), (g_ref,) = refs[:4], refs[4:8], refs[8:10], refs[10:]
    shifted = {}
    for which in range(2):
        full = jnp.concatenate([d[which] for d in d_refs], 0).astype(F32)
        for sy in range(2):
            for sz in range(2):
                shifted[which, sy, sz] = earlier(full, sy, sz).astype(BF)
    mine = pl.multiple_of(core_ref[0] * 64, 64)
    other = pl.multiple_of(64 - core_ref[0] * 64, 64)
    for c in range(4):
        for p, firsts in ((0, (1,)), (1, (2, 0))):
            total = None
            for k1 in firsts:
                for tap, sy, sz in taps_of(c):
                    at = (9 * k1 + tap) * 128
                    w = jnp.concatenate([w[:, at : at + 128] for w in w_refs], 0)
                    r = lax.dot_general(
                        w, shifted[1 if k1 == 0 else 0, sy, sz], (((0,), (0,)), ((), ())), preferred_element_type=F32
                    )
                    total = r if total is None else total + r
            g_ref[...] = total
            mine_ref[p, c] = g_ref[pl.ds(mine, 64), :]
            theirs_ref[p, c] = g_ref[pl.ds(other, 64), :]


def join_kernel(a_ref, b_ref, o_ref):
    matrix = split_matrix()
    for p in range(2):
        for h in range(2):
            at = slice(h * 128, h * 128 + 128)
            parts = [(a_ref[p, c, :, at] + b_ref[p, c, :, at]).astype(BF) for c in range(4)]
            r = lax.dot_general(
                jnp.concatenate(parts, 1), matrix, (((1,), (1,)), ((), ())), preferred_element_type=F32
            )
            o_ref[p, :, h * 512 : (h + 1) * 512] = r.astype(BF)


VMEM = pl.BlockSpec(memory_space=pltpu.VMEM)
SMEM = pl.BlockSpec(memory_space=pltpu.SMEM)


def call(kernel, outs, *args, scalars=0, scratch=()):
    shapes = [jax.ShapeDtypeStruct(s, t) for s, t in outs]
    result = pl.pallas_call(
        kernel,
        out_shape=shapes,
        in_specs=[SMEM] * scalars + [VMEM] * (len(args) - scalars),
        out_specs=[VMEM] * len(outs),
        scratch_shapes=list(scratch),
        compiler_params=PARAMS,
    )(*args)
    return result


def shift_space(a, by):
    return lax.ppermute(a, "space", [(i, i + by) for i in range(16) if 0 <= i + by < 16])


def to_x(a, d):
    return lax.ppermute(a, "chan", [(i, (i + 2 * d) % 8) for i in range(8)])


def over_y(a, by):
    pairs = []
    for i in range(32):
        dp, z, yh = i // 16, i % 16 // 2, i % 2
        y = (2 * yh + dp + by) % 4
        pairs.append((i, y % 2 * 16 + 2 * z + y // 2))
    return lax.ppermute(a, DS, pairs)


def to_partner(a):
    return lax.ppermute(a, "chan", [(i, i ^ 1) for i in range(8)])


def per_device(volumes, kernel, bias, act_grad):
    chan = lax.axis_index("chan")
    core = (chan % 2).astype(jnp.int32).reshape(1)
    x = (chan // 2).astype(jnp.int32).reshape(1)
    z_odd = ((lax.axis_index("space") // 2) % 2).astype(jnp.int32).reshape(1)

    q = ((lax.axis_index("space") % 2) * 2 + lax.axis_index("dp")).astype(jnp.int32).reshape(1)

    (cells,) = call(split_kernel, [((2, 4, 64, 256), BF)], volumes.reshape(2, 64, 1024))
    w_keep, w_send = call(
        core_pack_kernel, [((64, 6912), BF)] * 2, jnp.concatenate([core, x]), kernel, scalars=1
    )
    back, ahead = to_x(cells, 1), to_x(cells, 3)
    across = to_x(ahead[0], 3), to_x(back[1], 1)
    w_other = to_partner(w_send)
    outs = [((64, 256), F32)] * 2
    following, theirs = call(next_kernel, outs, cells, back, across[1], ahead, w_keep, w_other)
    following = shift_space(following + to_partner(theirs), 1)
    (x_own,) = call(in_order_kernel, [((4, 2, 4, 64, 256), BF)], x, cells, back, ahead, *across, scalars=1)
    packed = call(pack_kernel, [((64, 3456), BF)] * 4, x, kernel, scalars=1)
    *packed, x_own = lax.optimization_barrier((*packed, x_own))
    ring = lax.all_to_all(x_own, DS, 0, 0, axis_index_groups=Y_GROUPS)
    far = to_x(packed[2], 2)
    mine, theirs = call(forward_kernel, outs, x, x_own, w_keep, w_other, scalars=1)
    parts = (mine, to_partner(theirs), following)
    activation, dy_own, dy_copies = call(
        gelu_kernel,
        [((64, 256), BF), ((64, 256), BF), ((8, 64, 256), BF)],
        *parts,
        bias.reshape(64, 1),
        act_grad.reshape(64, 256),
    )
    ring, dy_own = lax.optimization_barrier((ring, dy_own))
    dy = lax.all_to_all(dy_copies, ALL, 0, 0, axis_index_groups=YC_GROUPS)
    edge = shift_space(ring[2:, 1], 2)
    dy_next = shift_space(dy_own, -1)
    (terms,) = call(
        filter_grad_kernel, [((16, 16, 896), BF)], dy, ring, edge, scratch=[pltpu.VMEM((4, 192, 1024), BF)]
    )
    far, dy_next, terms = lax.optimization_barrier((far, dy_next, terms))
    terms = lax.all_to_all(terms, ALL, 0, 0, axis_index_groups=ZC_GROUPS)
    both = jnp.stack([dy_own, dy_next])
    grads = [both] + [to_x(both, d) for d in range(1, 4)]
    *near, grads[1], grads[2], grads[3] = lax.optimization_barrier((packed[1], packed[3], *grads[1:]))
    grads[1], terms = lax.optimization_barrier((grads[1], terms))
    far = [to_x(near[0], 1), far, to_x(near[1], 3)]
    (terms,) = call(sum_z_kernel, [((8, 2, 16, 896), BF)], z_odd, terms, scalars=1)
    mine, theirs = call(
        input_grad_kernel,
        [((2, 4, 64, 256), F32), ((2, 4, 64, 256), F32)],
        core,
        packed[0],
        *far,
        *grads,
        scalars=1,
        scratch=[pltpu.VMEM((128, 256), F32)],
    )
    terms = lax.all_to_all(terms, DS, 0, 0, axis_index_groups=Z_GROUPS)
    theirs = to_partner(theirs)
    mine, theirs, terms = lax.optimization_barrier((mine, theirs, terms))
    half = call(cut_kernel, [((4, 2, 16, 896), BF)] * 2, terms)
    back = [over_y(half[0], 1), over_y(half[1], 1)]
    ahead = [over_y(half[0], -1), over_y(half[1], -1)]
    across = [over_y(back[0], 1), over_y(ahead[1], -1)]
    (grad_x,) = call(join_kernel, [((2, 64, 1024), BF)], mine, theirs)
    grad_w, grad_b = filter_out((0,), q, half)
    grad_w = filter_out((3, 1), q, back + ahead, grad_w)
    grad_w = filter_out((2,), q, across, grad_w)
    return (
        activation.reshape(1, 1, 64, 256),
        grad_x.reshape(1, 2, 64, 1024),
        grad_w,
        grad_b.reshape(64),
    )


def solution(mesh):
    in_specs = (
        P("dp", "space", "chan", None),
        P("chan", None),
        P("chan"),
        P("dp", "space", "chan", None),
    )
    out_specs = (
        P("dp", "space", "chan", None),
        P("dp", "space", "chan", None),
        P("chan", None),
        P("chan"),
    )
    return jax.shard_map(
        per_device, mesh=mesh, in_specs=in_specs, out_specs=out_specs, check_vma=False
    )
```

```python
import functools

import jax
import jax.numpy as jnp
import numpy as np
from jax import lax
from jax.experimental import pallas as pl
from jax.experimental.pallas import tpu as pltpu
from jax.sharding import PartitionSpec as P

BF = jnp.bfloat16
F32 = jnp.float32
DS = ("dp", "space")
ALL = ("dp", "space", "chan")
Y_GROUPS = [[dp * 16 + z * 2 + yh for yh in range(2) for dp in range(2)] for z in range(8)]
Z_GROUPS = [[dp * 16 + z * 2 + yh for z in range(7, -1, -1)] for yh in range(2) for dp in range(2)]
YC_GROUPS = [
    [((dp * 16 + z * 2 + yh) * 8 + 2 * x + core) for yh in range(2) for dp in range(2) for core in range(2)]
    for z in range(8)
    for x in range(4)
]
ZC_GROUPS = [
    [((dp * 16 + (z + 7) % 8 * 2 + yh) * 8 + 2 * x + core) for z in range(8) for core in range(2)]
    for yh in range(2)
    for dp in range(2)
    for x in range(4)
]
X_GROUPS = [[2 * x + core for x in range(4)] for core in range(2)]
TAP_OF = {(0, 0): 1, (1, 0): 2, (1, 1): 0}
PARAMS = pltpu.CompilerParams(vmem_limit_bytes=48 * 1024 * 1024)


def split_matrix():
    cell = lax.broadcasted_iota(jnp.int32, (512, 512), 0)
    lane = lax.broadcasted_iota(jnp.int32, (512, 512), 1)
    to = ((cell >> 5) & 1) * 256 + (cell & 1) * 128 + (cell >> 6) * 16 + ((cell & 31) >> 1)
    return jnp.where(lane == to, 1.0, 0.0).astype(BF)


def class_shifts(c):
    py, pz = c // 2, c % 2
    return [(sy, sz) for sy in range(py + 1) for sz in range(pz + 1)]


def taps_of(c):
    py, pz = c // 2, c % 2
    return [(TAP_OF[py, sy] * 3 + TAP_OF[pz, sz], sy, sz) for sy, sz in class_shifts(c)]


def lanes(shape):
    return lax.broadcasted_iota(jnp.int32, shape, 1)


def later(a, sy, sz):
    lane = lanes(a.shape)
    if sy:
        a = jnp.where(lane < 16, 0.0, pltpu.roll(a, 16, 1))
    if sz:
        a = jnp.where(lane % 16 == 0, 0.0, pltpu.roll(a, 1, 1))
    return a


def earlier(a, sy, sz):
    lane = lanes(a.shape)
    width = a.shape[1]
    if sy:
        a = jnp.where(lane % 256 >= 240, 0.0, pltpu.roll(a, width - 16, 1))
    if sz:
        a = jnp.where(lane % 16 == 15, 0.0, pltpu.roll(a, width - 1, 1))
    return a


def split_kernel(x_ref, o_ref):
    matrix = split_matrix()
    for p in range(2):
        for h in range(2):
            r = jnp.dot(x_ref[p, :, h * 512 : (h + 1) * 512], matrix, preferred_element_type=F32).astype(BF)
            for c in range(4):
                o_ref[p, c, :, h * 128 : (h + 1) * 128] = r[:, c * 128 : (c + 1) * 128]


def halves(a, b):
    low = lanes(a.shape) < 64
    return jnp.where(low, a, pltpu.roll(b, 64, 1)), jnp.where(low, pltpu.roll(a, 64, 1), b)


STEPS = (0, 3, 2, 1)


def core_pack_kernel(where_ref, w_ref, keep_ref, send_ref):
    first = where_ref[0] == 0
    starts = [lax.rem(where_ref[1] + step, 4) * 128 for step in STEPS]

    def block(tap, k):
        return w_ref[:, pl.ds(pl.multiple_of(tap * 512 + starts[k], 128), 128)].astype(F32)

    for tap in range(27):
        for pair in range(2):
            low, high = halves(block(tap, 2 * pair), block(tap, 2 * pair + 1))
            to = tap * 256 + pair * 128
            keep_ref[:, to : to + 128] = jnp.where(first, low, high).astype(BF)
            send_ref[:, to : to + 128] = jnp.where(first, high, low).astype(BF)


def in_order_kernel(x_ref, own_ref, back_ref, ahead_ref, across_0, across_1, o_ref):
    for step, ref in ((0, own_ref), (3, back_ref), (1, ahead_ref)):
        o_ref[lax.rem(x_ref[0] + step, 4)] = ref[...]
    for p, ref in enumerate((across_0, across_1)):
        o_ref[lax.rem(x_ref[0] + 2, 4), p] = ref[...]


def accumulate(sums, c, k1, w_ref, v_ref, cells):
    taps = taps_of(c)
    rows = []
    for tap, _, _ in taps:
        at = (9 * k1 + tap) * 256
        rows += [w_ref[:, at : at + 256], v_ref[:, at : at + 256]]
    r = jnp.dot(jnp.concatenate(rows, 0), jnp.concatenate(cells, 0), preferred_element_type=F32)
    for m, (_, sy, sz) in enumerate(taps):
        value = r[128 * m : 128 * m + 128]
        sums[sy, sz] = sums[sy, sz] + value if (sy, sz) in sums else value


def finish(sums, mine_ref, theirs_ref):
    total = sum(later(v, *s) for s, v in sums.items())
    mine_ref[...] = total[:64]
    theirs_ref[...] = total[64:]


def next_kernel(own_ref, back_ref, across_ref, ahead_ref, w_ref, v_ref, mine_ref, theirs_ref):
    sums = {}
    for c in range(4):
        accumulate(sums, c, 0, w_ref, v_ref, [own_ref[1, c], back_ref[1, c], across_ref[c], ahead_ref[1, c]])
    finish(sums, mine_ref, theirs_ref)


def forward_kernel(x_ref, all_ref, w_ref, v_ref, mine_ref, theirs_ref):
    sums = {}
    at = [lax.rem(x_ref[0] + step, 4) for step in STEPS]
    for c in range(4):
        for p in range(2):
            accumulate(sums, c, p + 1, w_ref, v_ref, [all_ref[i, p, c] for i in at])
    finish(sums, mine_ref, theirs_ref)


def gelu_kernel(a_ref, b_ref, c_ref, bias_ref, g_ref, act_ref, one_ref, dy_ref):
    u = ((a_ref[...] + b_ref[...]) + c_ref[...]) + bias_ref[...]
    root = float(np.sqrt(2 / np.pi))
    t = jnp.tanh(root * (u + 0.044715 * (u * u * u)))
    act_ref[...] = (0.5 * u * (1.0 + t)).astype(BF)
    slope = 0.5 * (1.0 + t) + 0.5 * u * (1.0 - t * t) * (root * (1.0 + 3 * 0.044715 * (u * u)))
    dy = (g_ref[...].astype(F32) * slope).astype(BF)
    one_ref[...] = dy
    for copy in range(8):
        dy_ref[copy] = dy


def with_pair(block, total):
    hi = total.astype(BF).astype(F32)
    lane = lanes(block.shape)
    pair = jnp.where(lane == 64, hi, jnp.where(lane == 65, total - hi, 0.0))
    return jnp.where(lane < 64, block, pair).astype(BF)


def filter_grad_kernel(dy_ref, x_ref, e_ref, o_ref, xs_ref):
    for c in range(4):
        for y in range(4):
            cells = slice(y * 256, y * 256 + 256)
            xs_ref[c, 0:64, cells] = x_ref[y, 0, c]
            xs_ref[c, 64:128, cells] = x_ref[y, 1, c]
            xs_ref[c, 128:192, cells] = e_ref[y, c] if y < 2 else x_ref[y - 2, 1, c]
    grads = jnp.concatenate(
        [jnp.concatenate([dy_ref[2 * y + core] for y in range(4)], 1) for core in range(2)], 0
    ).astype(F32)
    shifted = {(sy, sz): earlier(grads, sy, sz).astype(BF) for sy in range(2) for sz in range(2)}

    def put(n, block):
        h, at = divmod(n, 7)
        for core in range(2):
            for fb in range(4):
                row = core * 64 + fb * 16
                o_ref[(2 * fb + h + 1) % 8 * 2 + core, :, at * 128 : at * 128 + 128] = block[row : row + 16]

    firsts = {}
    for c in range(4):
        taps = taps_of(c)
        r = lax.dot_general(
            jnp.concatenate([shifted[sy, sz] for _, sy, sz in taps], 0),
            xs_ref[c],
            (((1,), (1,)), ((), ())),
            preferred_element_type=F32,
        )
        for n, (tap, _, _) in enumerate(taps):
            put(tap, r[128 * n : 128 * n + 128, 0:128].astype(BF))
            firsts[tap] = r[128 * n : 128 * n + 128, 128:192]
    for j in range(4):
        put(9 + j, jnp.concatenate([firsts[2 * j], firsts[2 * j + 1]], 1).astype(BF))
    last = jnp.concatenate([firsts[8], jnp.zeros((128, 64), F32)], 1)
    put(13, with_pair(last, jnp.sum(grads, 1, keepdims=True)))


def sum_z_kernel(odd_ref, r_ref, o_ref):
    for core in range(2):
        for at in range(0, 896, 128):
            total = sum(r_ref[2 * s + core, :, at : at + 128].astype(F32) for s in range(8))
            out = total.astype(BF)
            if at == 768:
                both = total[:, 64:65] + total[:, 65:66]
                out = jnp.where(odd_ref[0] == 1, with_pair(total, both).astype(F32), out.astype(F32)).astype(BF)
            for copy in range(8):
                o_ref[copy, core, :, at : at + 128] = out


def cut_kernel(r_ref, a_ref, b_ref):
    for i in range(4):
        a_ref[i] = r_ref[7 - i]
        b_ref[i] = r_ref[3 - i]


def place(first, second, store, bias):
    for z in range(8):
        fb, h = divmod(z, 2)
        ref = first if z < 4 else second
        rows = slice(fb * 16, fb * 16 + 16)
        for at in range(7):
            n = 7 * h + at
            a = ref[z % 4, 0, :, at * 128 : at * 128 + 128].astype(F32) * 0.5
            b = ref[z % 4, 1, :, at * 128 : at * 128 + 128].astype(F32) * 0.5
            low, high = halves(a, b)
            taps = (9 + n, 18 + n) if n < 9 else (2 * n - 18, 2 * n - 17)
            store(rows, taps[0], low)
            if n < 13:
                store(rows, taps[1], high)
            elif bias is not None:
                bias[rows, :] = a[:, 64:65] + a[:, 65:66]


def filter_out_kernel(sources, has_bias, q_ref, *refs):
    n = 2 * len(sources)
    ins = refs[:n]
    if has_bias:
        w_ref, b_ref, s_ref, sems = refs[n:]
    else:
        _, w_ref, s_ref, sems = refs[n:]
        b_ref = None
    copies = []
    for k, source in enumerate(sources):

        def store(rows, tap, value, k=k):
            s_ref[k, rows, tap * 128 : tap * 128 + 128] = value

        place(ins[2 * k], ins[2 * k + 1], store, b_ref)
        to = lax.rem(q_ref[0] + source, 4) * 128
        for tap in range(27):
            copies.append(
                pltpu.make_async_copy(
                    s_ref.at[k, :, pl.ds(tap * 128, 128)],
                    w_ref.at[:, pl.ds(pl.multiple_of(tap * 512 + to, 128), 128)],
                    sems.at[k * 27 + tap],
                )
            )
            copies[-1].start()
    for copy in copies:
        copy.wait()


def filter_out(sources, q, pieces, so_far=None):
    n = len(sources)
    anywhere = pl.BlockSpec(memory_space=pl.ANY)
    first = so_far is None
    shape = jax.ShapeDtypeStruct((64, 13824), F32)
    return pl.pallas_call(
        functools.partial(filter_out_kernel, sources, first),
        out_shape=[shape, jax.ShapeDtypeStruct((64, 1), F32)] if first else shape,
        in_specs=[SMEM] + [VMEM] * (2 * n) + ([] if first else [anywhere]),
        out_specs=[anywhere, VMEM] if first else anywhere,
        scratch_shapes=[pltpu.VMEM((n, 64, 3456), F32), pltpu.SemaphoreType.DMA((27 * n,))],
        input_output_aliases={} if first else {2 * n + 1: 0},
        compiler_params=PARAMS,
    )(q, *pieces, *([] if first else [so_far]))


def pack_kernel(x_ref, w_ref, *o_refs):
    for d in range(4):
        to = lax.rem(x_ref[0] + d, 4) * 128
        for tap in range(27):
            o_refs[d][:, tap * 128 : tap * 128 + 128] = w_ref[:, pl.ds(pl.multiple_of(tap * 512 + to, 128), 128)]


def input_grad_kernel(core_ref, *refs):
    w_refs, d_refs, (mine_ref, theirs_ref), (g_ref,) = refs[:4], refs[4:8], refs[8:10], refs[10:]
    shifted = {}
    for which in range(2):
        full = jnp.concatenate([d[which] for d in d_refs], 0).astype(F32)
        for sy in range(2):
            for sz in range(2):
                shifted[which, sy, sz] = earlier(full, sy, sz).astype(BF)
    mine = pl.multiple_of(core_ref[0] * 64, 64)
    other = pl.multiple_of(64 - core_ref[0] * 64, 64)
    for c in range(4):
        for p, firsts in ((0, (1,)), (1, (2, 0))):
            total = None
            for k1 in firsts:
                for tap, sy, sz in taps_of(c):
                    at = (9 * k1 + tap) * 128
                    w = jnp.concatenate([w[:, at : at + 128] for w in w_refs], 0)
                    r = lax.dot_general(
                        w, shifted[1 if k1 == 0 else 0, sy, sz], (((0,), (0,)), ((), ())), preferred_element_type=F32
                    )
                    total = r if total is None else total + r
            g_ref[...] = total
            mine_ref[p, c] = g_ref[pl.ds(mine, 64), :]
            theirs_ref[p, c] = g_ref[pl.ds(other, 64), :]


def join_kernel(a_ref, b_ref, o_ref):
    matrix = split_matrix()
    for p in range(2):
        for h in range(2):
            at = slice(h * 128, h * 128 + 128)
            parts = [(a_ref[p, c, :, at] + b_ref[p, c, :, at]).astype(BF) for c in range(4)]
            r = lax.dot_general(
                jnp.concatenate(parts, 1), matrix, (((1,), (1,)), ((), ())), preferred_element_type=F32
            )
            o_ref[p, :, h * 512 : (h + 1) * 512] = r.astype(BF)


VMEM = pl.BlockSpec(memory_space=pltpu.VMEM)
SMEM = pl.BlockSpec(memory_space=pltpu.SMEM)


def call(kernel, outs, *args, scalars=0, scratch=()):
    shapes = [jax.ShapeDtypeStruct(s, t) for s, t in outs]
    result = pl.pallas_call(
        kernel,
        out_shape=shapes,
        in_specs=[SMEM] * scalars + [VMEM] * (len(args) - scalars),
        out_specs=[VMEM] * len(outs),
        scratch_shapes=list(scratch),
        compiler_params=PARAMS,
    )(*args)
    return result


def shift_space(a, by):
    return lax.ppermute(a, "space", [(i, i + by) for i in range(16) if 0 <= i + by < 16])


def to_x(a, d):
    return lax.ppermute(a, "chan", [(i, (i + 2 * d) % 8) for i in range(8)])


def over_y(a, by):
    pairs = []
    for i in range(32):
        dp, z, yh = i // 16, i % 16 // 2, i % 2
        y = (2 * yh + dp + by) % 4
        pairs.append((i, y % 2 * 16 + 2 * z + y // 2))
    return lax.ppermute(a, DS, pairs)


def to_partner(a):
    return lax.ppermute(a, "chan", [(i, i ^ 1) for i in range(8)])


def per_device(volumes, kernel, bias, act_grad):
    chan = lax.axis_index("chan")
    core = (chan % 2).astype(jnp.int32).reshape(1)
    x = (chan // 2).astype(jnp.int32).reshape(1)
    z_odd = ((lax.axis_index("space") // 2) % 2).astype(jnp.int32).reshape(1)

    q = ((lax.axis_index("space") % 2) * 2 + lax.axis_index("dp")).astype(jnp.int32).reshape(1)

    (cells,) = call(split_kernel, [((2, 4, 64, 256), BF)], volumes.reshape(2, 64, 1024))
    w_keep, w_send = call(
        core_pack_kernel, [((64, 6912), BF)] * 2, jnp.concatenate([core, x]), kernel, scalars=1
    )
    back, ahead = to_x(cells, 1), to_x(cells, 3)
    across = to_x(ahead[0], 3), to_x(back[1], 1)
    w_other = to_partner(w_send)
    outs = [((64, 256), F32)] * 2
    following, theirs = call(next_kernel, outs, cells, back, across[1], ahead, w_keep, w_other)
    following = shift_space(following + to_partner(theirs), 1)
    (x_own,) = call(in_order_kernel, [((4, 2, 4, 64, 256), BF)], x, cells, back, ahead, *across, scalars=1)
    packed = call(pack_kernel, [((64, 3456), BF)] * 4, x, kernel, scalars=1)
    *packed, x_own = lax.optimization_barrier((*packed, x_own))
    ring = lax.all_to_all(x_own, DS, 0, 0, axis_index_groups=Y_GROUPS)
    far = to_x(packed[2], 2)
    mine, theirs = call(forward_kernel, outs, x, x_own, w_keep, w_other, scalars=1)
    parts = (mine, to_partner(theirs), following)
    activation, dy_own, dy_copies = call(
        gelu_kernel,
        [((64, 256), BF), ((64, 256), BF), ((8, 64, 256), BF)],
        *parts,
        bias.reshape(64, 1),
        act_grad.reshape(64, 256),
    )
    ring, dy_own = lax.optimization_barrier((ring, dy_own))
    dy = lax.all_to_all(dy_copies, ALL, 0, 0, axis_index_groups=YC_GROUPS)
    edge = shift_space(ring[2:, 1], 2)
    dy_next = shift_space(dy_own, -1)
    (terms,) = call(
        filter_grad_kernel, [((16, 16, 896), BF)], dy, ring, edge, scratch=[pltpu.VMEM((4, 192, 1024), BF)]
    )
    far, dy_next, terms = lax.optimization_barrier((far, dy_next, terms))
    terms = lax.all_to_all(terms, ALL, 0, 0, axis_index_groups=ZC_GROUPS)
    both = jnp.stack([dy_own, dy_next])
    grads = [both] + [to_x(both, d) for d in range(1, 4)]
    *near, grads[1], grads[2], grads[3] = lax.optimization_barrier((packed[1], packed[3], *grads[1:]))
    grads[1], terms = lax.optimization_barrier((grads[1], terms))
    far = [to_x(near[0], 1), far, to_x(near[1], 3)]
    (terms,) = call(sum_z_kernel, [((8, 2, 16, 896), BF)], z_odd, terms, scalars=1)
    mine, theirs = call(
        input_grad_kernel,
        [((2, 4, 64, 256), F32), ((2, 4, 64, 256), F32)],
        core,
        packed[0],
        *far,
        *grads,
        scalars=1,
        scratch=[pltpu.VMEM((128, 256), F32)],
    )
    terms = lax.all_to_all(terms, DS, 0, 0, axis_index_groups=Z_GROUPS)
    theirs = to_partner(theirs)
    mine, theirs, terms = lax.optimization_barrier((mine, theirs, terms))
    half = call(cut_kernel, [((4, 2, 16, 896), BF)] * 2, terms)
    back = [over_y(half[0], 1), over_y(half[1], 1)]
    ahead = [over_y(half[0], -1), over_y(half[1], -1)]
    across = [over_y(back[0], 1), over_y(ahead[1], -1)]
    (grad_x,) = call(join_kernel, [((2, 64, 1024), BF)], mine, theirs)
    grad_w, grad_b = filter_out((0,), q, half)
    grad_w = filter_out((3, 1), q, back + ahead, grad_w)
    grad_w = filter_out((2,), q, across, grad_w)
    return (
        activation.reshape(1, 1, 64, 256),
        grad_x.reshape(1, 2, 64, 1024),
        grad_w,
        grad_b.reshape(64),
    )


def solution(mesh):
    in_specs = (
        P("dp", "space", "chan", None),
        P("chan", None),
        P("chan"),
        P("dp", "space", "chan", None),
    )
    out_specs = (
        P("dp", "space", "chan", None),
        P("dp", "space", "chan", None),
        P("chan", None),
        P("chan"),
    )
    return jax.shard_map(
        per_device, mesh=mesh, in_specs=in_specs, out_specs=out_specs, check_vma=False
    )
```

```python
import functools

import jax
import jax.numpy as jnp
import numpy as np
from jax import lax
from jax.experimental import pallas as pl
from jax.experimental.pallas import tpu as pltpu
from jax.sharding import PartitionSpec as P

BF = jnp.bfloat16
F32 = jnp.float32
DS = ("dp", "space")
ALL = ("dp", "space", "chan")
Y_GROUPS = [[dp * 16 + z * 2 + yh for yh in range(2) for dp in range(2)] for z in range(8)]
Z_GROUPS = [[dp * 16 + z * 2 + yh for z in range(7, -1, -1)] for yh in range(2) for dp in range(2)]
YC_GROUPS = [
    [((dp * 16 + z * 2 + yh) * 8 + 2 * x + core) for yh in (1, 0) for dp in (1, 0) for core in (1, 0)]
    for z in range(8)
    for x in range(4)
]
ZC_GROUPS = [
    [((dp * 16 + (z + 7) % 8 * 2 + yh) * 8 + 2 * x + core) for z in range(8) for core in range(2)]
    for yh in range(2)
    for dp in range(2)
    for x in range(4)
]
X_GROUPS = [[2 * x + core for x in range(4)] for core in range(2)]
TAP_OF = {(0, 0): 1, (1, 0): 2, (1, 1): 0}
PARAMS = pltpu.CompilerParams(vmem_limit_bytes=48 * 1024 * 1024)


def split_matrix():
    cell = lax.broadcasted_iota(jnp.int32, (512, 512), 0)
    lane = lax.broadcasted_iota(jnp.int32, (512, 512), 1)
    to = ((cell >> 5) & 1) * 256 + (cell & 1) * 128 + (cell >> 6) * 16 + ((cell & 31) >> 1)
    return jnp.where(lane == to, 1.0, 0.0).astype(BF)


def class_shifts(c):
    py, pz = c // 2, c % 2
    return [(sy, sz) for sy in range(py + 1) for sz in range(pz + 1)]


def taps_of(c):
    py, pz = c // 2, c % 2
    return [(TAP_OF[py, sy] * 3 + TAP_OF[pz, sz], sy, sz) for sy, sz in class_shifts(c)]


def lanes(shape):
    return lax.broadcasted_iota(jnp.int32, shape, 1)


def later(a, sy, sz):
    lane = lanes(a.shape)
    if sy:
        a = jnp.where(lane < 16, 0.0, pltpu.roll(a, 16, 1))
    if sz:
        a = jnp.where(lane % 16 == 0, 0.0, pltpu.roll(a, 1, 1))
    return a


def earlier(a, sy, sz):
    lane = lanes(a.shape)
    width = a.shape[1]
    if sy:
        a = jnp.where(lane % 256 >= 240, 0.0, pltpu.roll(a, width - 16, 1))
    if sz:
        a = jnp.where(lane % 16 == 15, 0.0, pltpu.roll(a, width - 1, 1))
    return a


def split_kernel(x_ref, o_ref):
    matrix = split_matrix()
    for p in range(2):
        for h in range(2):
            r = jnp.dot(x_ref[p, :, h * 512 : (h + 1) * 512], matrix, preferred_element_type=F32).astype(BF)
            for c in range(4):
                o_ref[p, c, :, h * 128 : (h + 1) * 128] = r[:, c * 128 : (c + 1) * 128]


def halves(a, b):
    low = lanes(a.shape) < 64
    return jnp.where(low, a, pltpu.roll(b, 64, 1)), jnp.where(low, pltpu.roll(a, 64, 1), b)


STEPS = (0, 3, 2, 1)


def core_pack_kernel(where_ref, w_ref, keep_ref, send_ref):
    first = where_ref[0] == 0
    starts = [lax.rem(where_ref[1] + step, 4) * 128 for step in STEPS]

    def block(tap, k):
        return w_ref[:, pl.ds(pl.multiple_of(tap * 512 + starts[k], 128), 128)].astype(F32)

    for tap in range(27):
        for pair in range(2):
            low, high = halves(block(tap, 2 * pair), block(tap, 2 * pair + 1))
            to = tap * 256 + pair * 128
            keep_ref[:, to : to + 128] = jnp.where(first, low, high).astype(BF)
            send_ref[:, to : to + 128] = jnp.where(first, high, low).astype(BF)


def in_order_kernel(x_ref, own_ref, back_ref, ahead_ref, across_0, across_1, o_ref):
    for step, ref in ((0, own_ref), (3, back_ref), (1, ahead_ref)):
        o_ref[lax.rem(x_ref[0] + step, 4)] = ref[...]
    for p, ref in enumerate((across_0, across_1)):
        o_ref[lax.rem(x_ref[0] + 2, 4), p] = ref[...]


def accumulate(sums, c, k1, w_ref, v_ref, cells):
    taps = taps_of(c)
    rows = []
    for tap, _, _ in taps:
        at = (9 * k1 + tap) * 256
        rows += [w_ref[:, at : at + 256], v_ref[:, at : at + 256]]
    r = jnp.dot(jnp.concatenate(rows, 0), jnp.concatenate(cells, 0), preferred_element_type=F32)
    for m, (_, sy, sz) in enumerate(taps):
        value = r[128 * m : 128 * m + 128]
        sums[sy, sz] = sums[sy, sz] + value if (sy, sz) in sums else value


def finish(sums, mine_ref, theirs_ref):
    total = sum(later(v, *s) for s, v in sums.items())
    mine_ref[...] = total[:64]
    theirs_ref[...] = total[64:]


def next_kernel(own_ref, back_ref, across_ref, ahead_ref, w_ref, v_ref, mine_ref, theirs_ref):
    sums = {}
    for c in range(4):
        accumulate(sums, c, 0, w_ref, v_ref, [own_ref[1, c], back_ref[1, c], across_ref[c], ahead_ref[1, c]])
    finish(sums, mine_ref, theirs_ref)


def forward_kernel(x_ref, all_ref, w_ref, v_ref, mine_ref, theirs_ref):
    sums = {}
    at = [lax.rem(x_ref[0] + step, 4) for step in STEPS]
    for c in range(4):
        for p in range(2):
            accumulate(sums, c, p + 1, w_ref, v_ref, [all_ref[i, p, c] for i in at])
    finish(sums, mine_ref, theirs_ref)


def gelu_kernel(a_ref, b_ref, c_ref, bias_ref, g_ref, act_ref, one_ref, dy_ref):
    u = ((a_ref[...] + b_ref[...]) + c_ref[...]) + bias_ref[...]
    root = float(np.sqrt(2 / np.pi))
    t = jnp.tanh(root * (u + 0.044715 * (u * u * u)))
    act_ref[...] = (0.5 * u * (1.0 + t)).astype(BF)
    slope = 0.5 * (1.0 + t) + 0.5 * u * (1.0 - t * t) * (root * (1.0 + 3 * 0.044715 * (u * u)))
    dy = (g_ref[...].astype(F32) * slope).astype(BF)
    one_ref[...] = dy
    for copy in range(8):
        dy_ref[copy] = dy


def with_pair(block, total):
    hi = total.astype(BF).astype(F32)
    lane = lanes(block.shape)
    pair = jnp.where(lane == 64, hi, jnp.where(lane == 65, total - hi, 0.0))
    return jnp.where(lane < 64, block, pair).astype(BF)


def filter_grad_kernel(dy_ref, x_ref, e_ref, o_ref, xs_ref):
    for c in range(4):
        for y in range(4):
            cells = slice(y * 256, y * 256 + 256)
            xs_ref[c, 0:64, cells] = x_ref[y, 0, c]
            xs_ref[c, 64:128, cells] = x_ref[y, 1, c]
            xs_ref[c, 128:192, cells] = e_ref[y, c] if y < 2 else x_ref[y - 2, 1, c]
    grads = jnp.concatenate(
        [jnp.concatenate([dy_ref[7 - 2 * y - core] for y in range(4)], 1) for core in range(2)], 0
    ).astype(F32)
    shifted = {(sy, sz): earlier(grads, sy, sz).astype(BF) for sy in range(2) for sz in range(2)}

    def put(n, block):
        h, at = divmod(n, 7)
        for core in range(2):
            for fb in range(4):
                row = core * 64 + fb * 16
                o_ref[(2 * fb + h + 1) % 8 * 2 + core, :, at * 128 : at * 128 + 128] = block[row : row + 16]

    firsts = {}
    for c in range(4):
        taps = taps_of(c)
        r = lax.dot_general(
            jnp.concatenate([shifted[sy, sz] for _, sy, sz in taps], 0),
            xs_ref[c],
            (((1,), (1,)), ((), ())),
            preferred_element_type=F32,
        )
        for n, (tap, _, _) in enumerate(taps):
            put(tap, r[128 * n : 128 * n + 128, 0:128].astype(BF))
            firsts[tap] = r[128 * n : 128 * n + 128, 128:192]
    for j in range(4):
        put(9 + j, jnp.concatenate([firsts[2 * j], firsts[2 * j + 1]], 1).astype(BF))
    last = jnp.concatenate([firsts[8], jnp.zeros((128, 64), F32)], 1)
    put(13, with_pair(last, jnp.sum(grads, 1, keepdims=True)))


def sum_z_kernel(odd_ref, r_ref, o_ref):
    for core in range(2):
        for at in range(0, 896, 128):
            total = sum(r_ref[2 * s + core, :, at : at + 128].astype(F32) for s in range(8))
            out = total.astype(BF)
            if at == 768:
                both = total[:, 64:65] + total[:, 65:66]
                out = jnp.where(odd_ref[0] == 1, with_pair(total, both).astype(F32), out.astype(F32)).astype(BF)
            for copy in range(8):
                o_ref[copy, core, :, at : at + 128] = out


def cut_kernel(r_ref, a_ref, b_ref):
    for i in range(4):
        a_ref[i] = r_ref[7 - i]
        b_ref[i] = r_ref[3 - i]


def place(first, second, store, bias):
    for z in range(8):
        fb, h = divmod(z, 2)
        ref = first if z < 4 else second
        rows = slice(fb * 16, fb * 16 + 16)
        for at in range(7):
            n = 7 * h + at
            a = ref[z % 4, 0, :, at * 128 : at * 128 + 128].astype(F32) * 0.5
            b = ref[z % 4, 1, :, at * 128 : at * 128 + 128].astype(F32) * 0.5
            low, high = halves(a, b)
            taps = (9 + n, 18 + n) if n < 9 else (2 * n - 18, 2 * n - 17)
            store(rows, taps[0], low)
            if n < 13:
                store(rows, taps[1], high)
            elif bias is not None:
                bias[rows, :] = a[:, 64:65] + a[:, 65:66]


def filter_out_kernel(sources, has_bias, q_ref, *refs):
    n = 2 * len(sources)
    ins = refs[:n]
    if has_bias:
        w_ref, b_ref, s_ref, sems = refs[n:]
    else:
        _, w_ref, s_ref, sems = refs[n:]
        b_ref = None
    copies = []
    for k, source in enumerate(sources):

        def store(rows, tap, value, k=k):
            s_ref[k, rows, tap * 128 : tap * 128 + 128] = value

        place(ins[2 * k], ins[2 * k + 1], store, b_ref)
        to = lax.rem(q_ref[0] + source, 4) * 128
        for tap in range(27):
            copies.append(
                pltpu.make_async_copy(
                    s_ref.at[k, :, pl.ds(tap * 128, 128)],
                    w_ref.at[:, pl.ds(pl.multiple_of(tap * 512 + to, 128), 128)],
                    sems.at[k * 27 + tap],
                )
            )
            copies[-1].start()
    for copy in copies:
        copy.wait()


def filter_out(sources, q, pieces, so_far=None):
    n = len(sources)
    anywhere = pl.BlockSpec(memory_space=pl.ANY)
    first = so_far is None
    shape = jax.ShapeDtypeStruct((64, 13824), F32)
    return pl.pallas_call(
        functools.partial(filter_out_kernel, sources, first),
        out_shape=[shape, jax.ShapeDtypeStruct((64, 1), F32)] if first else shape,
        in_specs=[SMEM] + [VMEM] * (2 * n) + ([] if first else [anywhere]),
        out_specs=[anywhere, VMEM] if first else anywhere,
        scratch_shapes=[pltpu.VMEM((n, 64, 3456), F32), pltpu.SemaphoreType.DMA((27 * n,))],
        input_output_aliases={} if first else {2 * n + 1: 0},
        compiler_params=PARAMS,
    )(q, *pieces, *([] if first else [so_far]))


def pack_kernel(x_ref, w_ref, *o_refs):
    for d in range(4):
        to = lax.rem(x_ref[0] + d, 4) * 128
        for tap in range(27):
            o_refs[d][:, tap * 128 : tap * 128 + 128] = w_ref[:, pl.ds(pl.multiple_of(tap * 512 + to, 128), 128)]


def input_grad_kernel(core_ref, *refs):
    w_refs, d_refs, (mine_ref, theirs_ref), (g_ref,) = refs[:4], refs[4:8], refs[8:10], refs[10:]
    shifted = {}
    for which in range(2):
        full = jnp.concatenate([d[which] for d in d_refs], 0).astype(F32)
        for sy in range(2):
            for sz in range(2):
                shifted[which, sy, sz] = earlier(full, sy, sz).astype(BF)
    mine = pl.multiple_of(core_ref[0] * 64, 64)
    other = pl.multiple_of(64 - core_ref[0] * 64, 64)
    for c in range(4):
        for p, firsts in ((0, (1,)), (1, (2, 0))):
            total = None
            for k1 in firsts:
                for tap, sy, sz in taps_of(c):
                    at = (9 * k1 + tap) * 128
                    w = jnp.concatenate([w[:, at : at + 128] for w in w_refs], 0)
                    r = lax.dot_general(
                        w, shifted[1 if k1 == 0 else 0, sy, sz], (((0,), (0,)), ((), ())), preferred_element_type=F32
                    )
                    total = r if total is None else total + r
            g_ref[...] = total
            mine_ref[p, c] = g_ref[pl.ds(mine, 64), :]
            theirs_ref[p, c] = g_ref[pl.ds(other, 64), :]


def join_kernel(a_ref, b_ref, o_ref):
    matrix = split_matrix()
    for p in range(2):
        for h in range(2):
            at = slice(h * 128, h * 128 + 128)
            parts = [(a_ref[p, c, :, at] + b_ref[p, c, :, at]).astype(BF) for c in range(4)]
            r = lax.dot_general(
                jnp.concatenate(parts, 1), matrix, (((1,), (1,)), ((), ())), preferred_element_type=F32
            )
            o_ref[p, :, h * 512 : (h + 1) * 512] = r.astype(BF)


VMEM = pl.BlockSpec(memory_space=pltpu.VMEM)
SMEM = pl.BlockSpec(memory_space=pltpu.SMEM)


def call(kernel, outs, *args, scalars=0, scratch=()):
    shapes = [jax.ShapeDtypeStruct(s, t) for s, t in outs]
    result = pl.pallas_call(
        kernel,
        out_shape=shapes,
        in_specs=[SMEM] * scalars + [VMEM] * (len(args) - scalars),
        out_specs=[VMEM] * len(outs),
        scratch_shapes=list(scratch),
        compiler_params=PARAMS,
    )(*args)
    return result


def shift_space(a, by):
    return lax.ppermute(a, "space", [(i, i + by) for i in range(16) if 0 <= i + by < 16])


def to_x(a, d):
    return lax.ppermute(a, "chan", [(i, (i + 2 * d) % 8) for i in range(8)])


def over_y(a, by):
    pairs = []
    for i in range(32):
        dp, z, yh = i // 16, i % 16 // 2, i % 2
        y = (2 * yh + dp + by) % 4
        pairs.append((i, y % 2 * 16 + 2 * z + y // 2))
    return lax.ppermute(a, DS, pairs)


def to_partner(a):
    return lax.ppermute(a, "chan", [(i, i ^ 1) for i in range(8)])


def per_device(volumes, kernel, bias, act_grad):
    chan = lax.axis_index("chan")
    core = (chan % 2).astype(jnp.int32).reshape(1)
    x = (chan // 2).astype(jnp.int32).reshape(1)
    z_odd = ((lax.axis_index("space") // 2) % 2).astype(jnp.int32).reshape(1)

    q = ((lax.axis_index("space") % 2) * 2 + lax.axis_index("dp")).astype(jnp.int32).reshape(1)

    (cells,) = call(split_kernel, [((2, 4, 64, 256), BF)], volumes.reshape(2, 64, 1024))
    w_keep, w_send = call(
        core_pack_kernel, [((64, 6912), BF)] * 2, jnp.concatenate([core, x]), kernel, scalars=1
    )
    back, ahead = to_x(cells, 1), to_x(cells, 3)
    across = to_x(ahead[0], 3), to_x(back[1], 1)
    w_other = to_partner(w_send)
    outs = [((64, 256), F32)] * 2
    following, theirs = call(next_kernel, outs, cells, back, across[1], ahead, w_keep, w_other)
    following = shift_space(following + to_partner(theirs), 1)
    (x_own,) = call(in_order_kernel, [((4, 2, 4, 64, 256), BF)], x, cells, back, ahead, *across, scalars=1)
    packed = call(pack_kernel, [((64, 3456), BF)] * 4, x, kernel, scalars=1)
    *packed, x_own = lax.optimization_barrier((*packed, x_own))
    ring = lax.all_to_all(x_own, DS, 0, 0, axis_index_groups=Y_GROUPS)
    far = to_x(packed[2], 2)
    mine, theirs = call(forward_kernel, outs, x, x_own, w_keep, w_other, scalars=1)
    parts = (mine, to_partner(theirs), following)
    activation, dy_own, dy_copies = call(
        gelu_kernel,
        [((64, 256), BF), ((64, 256), BF), ((8, 64, 256), BF)],
        *parts,
        bias.reshape(64, 1),
        act_grad.reshape(64, 256),
    )
    ring, dy_own = lax.optimization_barrier((ring, dy_own))
    dy = lax.all_to_all(dy_copies, ALL, 0, 0, axis_index_groups=YC_GROUPS)
    edge = shift_space(ring[2:, 1], 2)
    dy_next = shift_space(dy_own, -1)
    (terms,) = call(
        filter_grad_kernel, [((16, 16, 896), BF)], dy, ring, edge, scratch=[pltpu.VMEM((4, 192, 1024), BF)]
    )
    far, dy_next, terms = lax.optimization_barrier((far, dy_next, terms))
    terms = lax.all_to_all(terms, ALL, 0, 0, axis_index_groups=ZC_GROUPS)
    both = jnp.stack([dy_own, dy_next])
    grads = [both] + [to_x(both, d) for d in range(1, 4)]
    *near, grads[1], grads[2], grads[3] = lax.optimization_barrier((packed[1], packed[3], *grads[1:]))
    grads[1], terms = lax.optimization_barrier((grads[1], terms))
    far = [to_x(near[0], 1), far, to_x(near[1], 3)]
    (terms,) = call(sum_z_kernel, [((8, 2, 16, 896), BF)], z_odd, terms, scalars=1)
    mine, theirs = call(
        input_grad_kernel,
        [((2, 4, 64, 256), F32), ((2, 4, 64, 256), F32)],
        core,
        packed[0],
        *far,
        *grads,
        scalars=1,
        scratch=[pltpu.VMEM((128, 256), F32)],
    )
    terms = lax.all_to_all(terms, DS, 0, 0, axis_index_groups=Z_GROUPS)
    theirs = to_partner(theirs)
    mine, theirs, terms = lax.optimization_barrier((mine, theirs, terms))
    half = call(cut_kernel, [((4, 2, 16, 896), BF)] * 2, terms)
    back = [over_y(half[0], 1), over_y(half[1], 1)]
    ahead = [over_y(half[0], -1), over_y(half[1], -1)]
    across = [over_y(back[0], 1), over_y(ahead[1], -1)]
    (grad_x,) = call(join_kernel, [((2, 64, 1024), BF)], mine, theirs)
    grad_w, grad_b = filter_out((0,), q, half)
    grad_w = filter_out((3, 1), q, back + ahead, grad_w)
    grad_w = filter_out((2,), q, across, grad_w)
    return (
        activation.reshape(1, 1, 64, 256),
        grad_x.reshape(1, 2, 64, 1024),
        grad_w,
        grad_b.reshape(64),
    )


def solution(mesh):
    in_specs = (
        P("dp", "space", "chan", None),
        P("chan", None),
        P("chan"),
        P("dp", "space", "chan", None),
    )
    out_specs = (
        P("dp", "space", "chan", None),
        P("dp", "space", "chan", None),
        P("chan", None),
        P("chan"),
    )
    return jax.shard_map(
        per_device, mesh=mesh, in_specs=in_specs, out_specs=out_specs, check_vma=False
    )
```
